32 devices in a mesh: grp: 2 (over y), gx: 4 (over x, core), gy: 4 (over z).
Axes of the slice: x: 2, y: 2, z: 4, core: 2. Of those that a mesh axis runs over, the one named last changes fastest.
Arguments:
- permeability: float32 [8192, 512], P(('grp', 'gx'), 'gy'), parts along dimension 0, may hold values from 0.01 to 100
- support: int32 [256, 16, 36], P(('grp', 'gx'), 'gy'), parts along dimension 0, may hold values 0 or 1
Outputs:
- basis: float32 [256, 16, 36, 256], P(('grp', 'gx'), 'gy'), parts along dimension 0
The draws below stay inside these ranges and needn't reach their ends.
There are 2 independent parts, one for each index of `grp`. The reference program is written for one: setup_inputs(seed, part) draws one part's arguments, and reference() takes and returns one part's arrays. A program takes and returns all parts, laid end to end along the dimension named above; each array names one. Nothing has to cross between parts.
Inputs may be any that keep to these rules, and one draw needn't show every extreme that they name: 0 or 1 for each tile of the 6 x 6 around a block; the block's own 2 x 2 tiles are in the support whatever their entry.
All inputs are finite; a program needn't handle non-finite values.
Results may differ from the reference program's by a relative error of at most 0.00002.
Values sent between devices are 32-bit elements; how exact they have to be, the bound alone decides.
No kernel may reach another device: no remote copies, remote signals or barrier semaphores. Data moves between devices by JAX's collectives and lax.ppermute only.
A program may use at most 192 MiB of HBM per device.

```python
import jax
import jax.numpy as jnp

ITERS = 4
NX = 4096
NY = 512
NBX = 128
NBY = 16


def draw_permeability(key, part):
    key = jax.random.fold_in(key, 11)
    cell_key = jax.random.fold_in(key, 0)
    exponent = jax.random.uniform(cell_key, (NX, NY), jnp.float32, -2.0, 2.0)
    values = jnp.exp(exponent * jnp.float32(2.302585093))
    return jnp.clip(values, 0.01, 100.0).astype(jnp.float32)


def set_ends(array, rng, low, top_value):
    place = [jax.random.randint(jax.random.fold_in(rng, axis), (), 0, length) for axis, length in enumerate(array.shape)]
    longest = array.shape.index(max(array.shape))
    neighbour = place[:longest] + [(place[longest] + 1) % array.shape[longest]] + place[longest + 1:]
    return array.at[tuple(place)].set(low).at[tuple(neighbour)].set(top_value)


def setup_inputs(seed: int = 0, part: int = 0) -> dict:
    streams_of = jax.random.split(jax.random.key(seed), 3)
    part_keys = jax.random.split(jax.random.fold_in(streams_of[2], part), 3)
    permeability = draw_permeability(jax.random.fold_in(jax.random.fold_in(streams_of[2], part), 71), part)
    support = set_ends((jax.random.randint(part_keys[1], (NBX, NBY, 36), 0, 3) < 2).astype(jnp.int32), jax.random.fold_in(part_keys[1], 1), 0, 1)
    return dict(permeability=permeability, support=support)


OMEGA = 2.0 / 3.0


def face_fields(haloed, first_x, first_y, grid_rows, grid_cols):
    rows_h, cols_h = haloed.shape
    coord_x = first_x - 33 + jnp.arange(rows_h, dtype=jnp.int32)
    coord_y = first_y - 33 + jnp.arange(cols_h, dtype=jnp.int32)
    inside = ((coord_x >= 0) & (coord_x < grid_rows))[:, None] & ((coord_y >= 0) & (coord_y < grid_cols))[None, :]
    perm = jnp.where(inside, haloed, jnp.float32(1.0))
    both_x = inside[:-1] & inside[1:]
    face_x = jnp.where(both_x, 2.0 * perm[:-1] * perm[1:] / (perm[:-1] + perm[1:]), jnp.float32(0.0))
    both_y = inside[:, :-1] & inside[:, 1:]
    face_y = jnp.where(both_y, 2.0 * perm[:, :-1] * perm[:, 1:] / (perm[:, :-1] + perm[:, 1:]), jnp.float32(0.0))
    west = face_x[:-1, 1:-1]
    east = face_x[1:, 1:-1]
    south = face_y[1:-1, :-1]
    north = face_y[1:-1, 1:]
    inside_ext = inside[1:-1, 1:-1]
    diag = jnp.where(inside_ext, west + east + south + north, jnp.float32(1.0))
    return west, east, south, north, diag, inside_ext


def windows(field):
    super_x = field.shape[0] // 32
    super_y = field.shape[1] // 32
    blocks_x = super_x - 2
    blocks_y = super_y - 2
    four = field.reshape(super_x, 32, super_y, 32)
    stacked_rows = []
    for row_off in range(3):
        pieces = [four[row_off:row_off + blocks_x, :, col_off:col_off + blocks_y, :] for col_off in range(3)]
        stacked_rows.append(jnp.stack(pieces, axis=3))
    joined = jnp.stack(stacked_rows, axis=1)
    return joined.transpose(0, 3, 1, 2, 4, 5).reshape(blocks_x, blocks_y, 96, 96)


def assemble(smoothed):
    blocks_x, blocks_y = smoothed.shape[0], smoothed.shape[1]
    split = smoothed.reshape(blocks_x, blocks_y, 3, 32, 3, 32)
    total = jnp.zeros((blocks_x + 2, 32, blocks_y + 2, 32), jnp.float32)
    for row_off in range(3):
        for col_off in range(3):
            piece = split[:, :, row_off, :, col_off, :].transpose(0, 2, 1, 3)
            total = total + jnp.pad(piece, ((row_off, 2 - row_off), (0, 0), (col_off, 2 - col_off), (0, 0)))
    return total.reshape((blocks_x + 2) * 32, (blocks_y + 2) * 32)


def masks(support, inside_win):
    blocks_x, blocks_y = support.shape[0], support.shape[1]
    offsets = jnp.arange(6, dtype=jnp.int32)
    own_row = (offsets >= 2) & (offsets <= 3)
    own_tiles = own_row[:, None] & own_row[None, :]
    tile_on = (support.reshape(blocks_x, blocks_y, 6, 6) == 1) | own_tiles[None, None]

    def expand(tiles):
        wide = jnp.broadcast_to(tiles[:, :, :, None, :, None], (blocks_x, blocks_y, 6, 16, 6, 16))
        return wide.reshape(blocks_x, blocks_y, 96, 96)

    cell_mask = expand(tile_on) & inside_win
    own_cells = expand(jnp.broadcast_to(own_tiles[None, None], (blocks_x, blocks_y, 6, 6))) & inside_win
    return cell_mask, own_cells


def smooth(values, west, east, south, north, diag, cell_mask):
    from_west = jnp.pad(values, ((0, 0), (0, 0), (1, 0), (0, 0)))[:, :, :-1, :]
    from_east = jnp.pad(values, ((0, 0), (0, 0), (0, 1), (0, 0)))[:, :, 1:, :]
    from_south = jnp.pad(values, ((0, 0), (0, 0), (0, 0), (1, 0)))[:, :, :, :-1]
    from_north = jnp.pad(values, ((0, 0), (0, 0), (0, 0), (0, 1)))[:, :, :, 1:]
    beside = west * from_west + east * from_east + south * from_south + north * from_north
    return jnp.where(cell_mask, (1.0 - OMEGA) * values + OMEGA * beside / diag, jnp.float32(0.0))


def to_tiles(values):
    blocks_x, blocks_y = values.shape[0], values.shape[1]
    split = values.reshape(blocks_x, blocks_y, 6, 16, 6, 16).transpose(0, 1, 2, 4, 3, 5)
    return split.reshape(blocks_x, blocks_y, 36, 256)


def reference(permeability, support):
    grid_rows, grid_cols = permeability.shape
    haloed = jnp.pad(permeability, 33)
    west, east, south, north, diag, inside_ext = face_fields(haloed, 0, 0, grid_rows, grid_cols)
    west_w, east_w, south_w, north_w, diag_w = [windows(field) for field in (west, east, south, north, diag)]
    inside_win = windows(inside_ext)
    cell_mask, own_cells = masks(support, inside_win)
    values = jnp.where(own_cells, jnp.float32(1.0), jnp.float32(0.0))
    for step in range(ITERS):
        smoothed = smooth(values, west_w, east_w, south_w, north_w, diag_w, cell_mask)
        extended = assemble(smoothed)
        totals = extended[32:-32, 32:-32]
        back = windows(jnp.pad(totals, 32))
        values = smoothed / jnp.where(inside_win, back, jnp.float32(1.0))
    return to_tiles(values)
```

```python
import jax
import jax.numpy as jnp
from jax import lax
from jax.experimental import pallas as pl
from jax.experimental.pallas import tpu as pltpu
from jax.sharding import PartitionSpec as P

ITERS = 4
SIDES = (-1, 0, 1)
TINY = 1e-30

SEGMENTS = 4
CHUNKS = 2
SEG_BLOCKS = 9
SEG_ROWS = 32 * SEG_BLOCKS
RIM = 8
HALO = 40
PITCH = 304
FIRST, LAST = RIM - (ITERS - 1), RIM + SEG_ROWS + (ITERS - 1)
SUP_PITCH = 40

f32 = jnp.float32


def lanes():
    return lax.broadcasted_iota(jnp.int32, (8, 128), 1)


def window_lane(label):
    lane = lanes()
    return lax.rem(lane + (80 - 32 * label), 96) // 16


def pack_kernel(perm_ref, sup_ref, up_ref, down_ref):
    rows = perm_ref.shape[0]
    half = rows // 2
    low = perm_ref[:half, :]
    high = perm_ref[half:, :]
    left = lax.broadcasted_iota(jnp.int32, (half, 128), 1) < 64
    up_ref[:half, :] = jnp.where(left, pltpu.roll(low, 64, 1), high)
    down_ref[:half, :] = jnp.where(left, low, pltpu.roll(high, 64, 1))
    blocks = sup_ref.shape[0]
    pad = jnp.zeros((blocks, 92), f32)
    wide = [
        jnp.concatenate([sup_ref[:, q, :].astype(f32), pad], axis=1) for q in range(4)
    ]
    up_ref[half:, :] = wide[1] + pltpu.roll(wide[2], 36, 1) + pltpu.roll(wide[3], 72, 1)
    down_ref[half:, :] = wide[0] + pltpu.roll(wide[1], 36, 1) + pltpu.roll(wide[2], 72, 1)


def pack(perm, support):
    rows = perm.shape[0]
    shape = jax.ShapeDtypeStruct((rows // 2 + support.shape[0], 128), f32)
    return pl.pallas_call(pack_kernel, out_shape=(shape, shape), name="pack")(perm, support)


def widen_kernel(perm_ref, sup_ref, left_ref, right_ref, field_ref, wide_ref, up_ref, down_ref):
    rows = perm_ref.shape[0]
    half = rows // 2
    lane = lax.broadcasted_iota(jnp.int32, (half, 128), 1)
    for part in range(2):
        own = perm_ref[part * half : (part + 1) * half, :]
        left = pltpu.roll(left_ref[:half, :], 112 if part == 0 else 48, 1)
        right = pltpu.roll(right_ref[:half, :], 80 if part == 0 else 16, 1)
        field_ref[0, part * half : (part + 1) * half, :] = jnp.where(
            lane < 48, left, pltpu.roll(own, 48, 1)
        )
        field_ref[1, part * half : (part + 1) * half, :] = jnp.where(
            lane < 80, pltpu.roll(own, 80, 1), right
        )
    for chunk in range(2):
        up_ref[chunk * HALO : (chunk + 1) * HALO, :] = field_ref[chunk, rows - HALO :, :]
        down_ref[chunk * HALO : (chunk + 1) * HALO, :] = field_ref[chunk, :HALO, :]
    blocks = sup_ref.shape[0]
    keep = lax.broadcasted_iota(jnp.int32, (blocks, 128), 1) < 36
    pad = jnp.zeros((blocks, 92), f32)
    for q in range(3):
        for source, place in ((left_ref, q), (right_ref, q + 7)):
            moved = source[half:, :] if q == 0 else pltpu.roll(source[half:, :], 128 - 36 * q, 1)
            wide_ref[place] = jnp.where(keep, moved, 0.0)
    for q in range(4):
        wide_ref[q + 3] = jnp.concatenate([sup_ref[:, q, :].astype(f32), pad], axis=1)
    for q in range(10):
        at = 2 * HALO + 4 * q
        up_ref[at : at + 4, :] = wide_ref[q, blocks - 4 :, :]
        down_ref[at : at + 4, :] = wide_ref[q, :4, :]


def widen(perm, support, from_left, from_right):
    rows, blocks = perm.shape[0], support.shape[0]
    edge = jax.ShapeDtypeStruct((2 * HALO + 40, 128), f32)
    return pl.pallas_call(
        widen_kernel,
        out_shape=(
            jax.ShapeDtypeStruct((2, rows, 128), f32),
            jax.ShapeDtypeStruct((10, blocks, 128), f32),
            edge,
            edge,
        ),
        name="widen",
    )(perm, support, from_left, from_right)


def row_of(field, r):
    return field[pl.ds(r, 8, stride=PITCH), :]


def build_masks(field, sup, near, mask):
    for q in range(7):
        for i in range(SEG_BLOCKS + 4):
            for chunk in range(CHUNKS):
                near[q, i, 4 * chunk : 4 * chunk + 4, :] = sup[
                    pl.ds((q + 3 * chunk) * SUP_PITCH + i, 4, stride=SEG_BLOCKS), :
                ]
    lane = lanes()

    def region(step, carry):
        for tr in range(2):
            tile = 2 * step + tr
            r = jnp.clip(RIM + 16 * (tile - 2), RIM - 1, RIM + SEG_ROWS)
            inside = row_of(field, r) > 0.0
            for dx in SIDES:
                a = 2 * (1 - dx) + tr
                for ly in range(3):
                    column = window_lane(ly)
                    entry = column + 6 * a
                    chosen = jnp.take_along_axis(near[ly, step + dx + 1], entry, axis=1)
                    later = jnp.take_along_axis(near[ly + 3, step + dx + 1], entry, axis=1)
                    chosen = jnp.where(lane >= 16 + 32 * ly, later, chosen)
                    if ly == 0:
                        last = jnp.take_along_axis(near[6, step + dx + 1], entry, axis=1)
                        chosen = jnp.where(lane >= 112, last, chosen)
                    on = chosen == 1.0
                    if dx == 0:
                        on = on | ((column >= 2) & (column <= 3))
                    mask[tile, 3 * (dx + 1) + ly] = jnp.where(on & inside, f32(1.0), f32(0.0))
        return carry

    lax.fori_loop(0, SEG_BLOCKS + 2, region, 0)


def build_faces(field, coef, values):
    lane = lanes()
    starts = [(lane == 16) | (lane == 112), lane == 48, lane == 80]
    ends = [(lane == 15) | (lane == 111), lane == 47, lane == 79]
    own = [(window_lane(ly) >= 2) & (window_lane(ly) <= 3) for ly in range(3)]
    zero = jnp.zeros((8, 128), f32)

    def face(p, q):
        return 2.0 * p * q / jnp.maximum(p + q, TINY)

    def rows(step, carry):
        here, west = carry
        for u in range(6):
            r = FIRST + 6 * step + u
            there = row_of(field, r + 1)
            east = face(here, there)
            south = face(here, pltpu.roll(here, 1, 1))
            north = pltpu.roll(south, 127, 1)
            scale = 2.0 / jnp.maximum(west + east + south + north, TINY)
            coef[0, r] = scale * west
            coef[1, r] = scale * east
            south = scale * south
            north = scale * north
            for ly in range(3):
                coef[2 + ly, r] = jnp.where(starts[ly], 0.0, south)
                coef[5 + ly, r] = jnp.where(ends[ly], 0.0, north)
            for ly in range(3):
                values[0, 3 + ly, r] = jnp.where(own[ly] & (here > 0.0), f32(1.0), f32(0.0))
                values[0, ly, r] = zero
                values[0, 6 + ly, r] = zero
            here, west = there, east
        return here, west

    first = row_of(field, FIRST)
    lax.fori_loop(0, (LAST - FIRST) // 6, rows, (first, face(row_of(field, FIRST - 1), first)))
    for r in (FIRST - 1, LAST):
        inside = row_of(field, r) > 0.0
        for label in range(9):
            values[0, label, r] = zero
            values[1, label, r] = zero
        for ly in range(3):
            values[0, 3 + ly, r] = jnp.where(own[ly] & inside, f32(1.0), f32(0.0))


def smooth_row(values, coef, mask, now, r, tile, first_row, last_row):
    west, east = coef[0, r], coef[1, r]
    smoothed = []
    total = None
    for dx in SIDES:
        for ly in range(3):
            label = 3 * (dx + 1) + ly
            here = values[now, label, r]
            term = here
            if not first_row:
                term = term + west * values[now, label, r - 1]
            elif dx < 1:
                term = term + west * values[now, label + 3, r - 1]
            if not last_row:
                term = term + east * values[now, label, r + 1]
            elif dx > -1:
                term = term + east * values[now, label - 3, r + 1]
            term = term + coef[2 + ly, r] * pltpu.roll(here, 1, 1)
            term = term + coef[5 + ly, r] * pltpu.roll(here, 127, 1)
            term = mask[tile, label] * term
            smoothed.append(term)
            total = term if total is None else total + term
    inverse = 1.0 / jnp.maximum(total, TINY)
    for label in range(9):
        values[1 - now, label, r] = smoothed[label] * inverse


def iterate(values, coef, mask):
    def iteration(count, carry):
        now = lax.rem(count, 2)
        for r in range(FIRST, RIM):
            smooth_row(values, coef, mask, now, r, 1, False, r == RIM - 1)

        def region(b, inner):
            for u in range(32):
                smooth_row(
                    values, coef, mask, now, RIM + 32 * b + u, 2 * b + 2 + u // 16, u == 0, u == 31
                )
            return inner

        lax.fori_loop(0, SEG_BLOCKS, region, 0)
        for r in range(RIM + SEG_ROWS, LAST):
            smooth_row(values, coef, mask, now, r, 2 * SEG_BLOCKS + 2, r == RIM + SEG_ROWS, False)
        return carry

    lax.fori_loop(0, ITERS, iteration, 0)


def swap_groups(rows):
    group = lanes() // 16
    rows = list(rows)
    for bit in (1, 2, 4):
        upper = (group & bit) != 0
        for i in range(8):
            if i & bit == 0:
                a, b = rows[i], rows[i + bit]
                rows[i] = jnp.where(upper, pltpu.roll(b, 16 * bit, 1), a)
                rows[i + bit] = jnp.where(upper, b, pltpu.roll(a, 128 - 16 * bit, 1))
    return rows


def to_tiles(values, moved, b, dx, wraps):
    place = b + dx - 1 + (SEG_BLOCKS if wraps else 0)
    for tr in range(2):
        a = 2 * (1 - dx) + tr
        for half in range(2):
            r = RIM + 32 * b + 16 * tr + 8 * half
            for ly in range(3):
                groups = swap_groups([values[0, 3 * (dx + 1) + ly, r + u] for u in range(8)])
                for g in range(1, 7):
                    column = (g - 1 - 2 * ly) % 6
                    shift = 7 if wraps else 0
                    if (ly == 1 and g <= 2) or (ly == 2 and g >= 5):
                        shift = (shift + 4) % 8
                    tile = groups[g] if shift == 0 else pltpu.roll(groups[g], shift, 0)
                    at = 8 * (6 * a + column)
                    moved[ly, half, place, at : at + 8, :] = tile


def emit(moved, out, i, k):
    for q, (array, at) in enumerate(((0, 0), (1, 0), (2, 4), (0, 4))):
        for half in range(2):
            for t in range(0, 36, 8):
                count = min(8, 36 - t)
                out[i + SEG_BLOCKS * k, q, t : t + count, 128 * half : 128 * half + 128] = moved[
                    array, half, i, pl.ds(8 * t + at + k, count, stride=8), :
                ]


def main_kernel(
    field_hbm, sup_ref, low_ref, high_ref, out, field, sup, near, mask, coef, values, moved, sem
):
    rows = field_hbm.shape[1]
    blocks = sup_ref.shape[1]
    copies = []
    for chunk in range(CHUNKS):
        for k in range(SEGMENTS):
            start = SEG_ROWS * k - HALO
            begin, end = max(start, 0), min(start + PITCH, rows)
            base = (4 * chunk + k) * PITCH
            copy = pltpu.make_async_copy(
                field_hbm.at[chunk, pl.ds(begin, end - begin), :],
                field.at[pl.ds(base + begin - start, end - begin), :],
                sem.at[4 * chunk + k],
            )
            copy.start()
            copies.append(copy)
    for q in range(10):
        at = q * SUP_PITCH
        sup[at : at + 3, :] = low_ref[2 * HALO + 4 * q + 1 : 2 * HALO + 4 * q + 4, :]
        sup[at + 3 : at + 3 + blocks, :] = sup_ref[q]
        sup[at + 3 + blocks : at + 6 + blocks, :] = high_ref[2 * HALO + 4 * q : 2 * HALO + 4 * q + 3, :]
        sup[at + 6 + blocks : at + SUP_PITCH, :] = jnp.zeros((SUP_PITCH - 6 - blocks, 128), f32)
    for copy in copies:
        copy.wait()
    for chunk in range(CHUNKS):
        base = 4 * chunk * PITCH
        field[base : base + HALO, :] = low_ref[chunk * HALO : (chunk + 1) * HALO, :]
        base = base + 3 * PITCH
        top = rows - (3 * SEG_ROWS - HALO)
        field[base + top : base + top + HALO, :] = high_ref[chunk * HALO : (chunk + 1) * HALO, :]
        field[base + top + HALO : base + PITCH, :] = jnp.zeros((PITCH - HALO - top, 128), f32)
    build_masks(field, sup, near, mask)
    build_faces(field, coef, values)
    iterate(values, coef, mask)
    for dx in SIDES:
        to_tiles(values, moved, 0, dx, dx < 1)
    for dx in SIDES:
        to_tiles(values, moved, 1, dx, dx < 0)

    def region(b, carry):
        for dx in SIDES:
            to_tiles(values, moved, b, dx, False)
        return carry

    lax.fori_loop(2, SEG_BLOCKS, region, 0)

    def block(i, carry):
        for k in range(3):
            emit(moved, out, i, k)
        return carry

    lax.fori_loop(0, SEG_BLOCKS, block, 0)

    def last_block(i, carry):
        emit(moved, out, i, 3)
        return carry

    lax.fori_loop(0, blocks - 3 * SEG_BLOCKS, last_block, 0)


def smooth(field, sup, low, high):
    blocks = sup.shape[1]
    vmem = pl.BlockSpec(memory_space=pltpu.VMEM)
    return pl.pallas_call(
        main_kernel,
        out_shape=jax.ShapeDtypeStruct((blocks, 4, 36, 256), f32),
        in_specs=[pl.BlockSpec(memory_space=pl.ANY), vmem, vmem, vmem],
        out_specs=vmem,
        scratch_shapes=[
            pltpu.VMEM((8 * PITCH, 128), f32),
            pltpu.VMEM((10 * SUP_PITCH, 128), f32),
            pltpu.VMEM((7, SEG_BLOCKS + 4, 8, 128), f32),
            pltpu.VMEM((2 * SEG_BLOCKS + 4, 9, 8, 128), f32),
            pltpu.VMEM((8, PITCH, 8, 128), f32),
            pltpu.VMEM((2, 9, PITCH, 8, 128), f32),
            pltpu.VMEM((3, 2, SEG_BLOCKS, 36 * 8, 128), f32),
            pltpu.SemaphoreType.DMA((8,)),
        ],
        compiler_params=pltpu.CompilerParams(vmem_limit_bytes=60 * 1024 * 1024),
        name="smooth",
    )(field, sup, low, high)


def neighbours(up, down, axis):
    count = lax.axis_size(axis)
    forward = [(i, i + 1) for i in range(count - 1)]
    backward = [(i + 1, i) for i in range(count - 1)]
    return lax.ppermute(up, axis, forward), lax.ppermute(down, axis, backward)


def body(permeability, support):
    up, down = pack(permeability, support)
    from_left, from_right = neighbours(up, down, "gy")
    field, sup, up, down = widen(permeability, support, from_left, from_right)
    low, high = neighbours(up, down, "gx")
    return smooth(field, sup, low, high)


def solution(mesh):
    return jax.shard_map(
        body,
        mesh=mesh,
        in_specs=(P(("grp", "gx"), "gy"), P(("grp", "gx"), "gy", None)),
        out_specs=P(("grp", "gx"), "gy", None, None),
        check_vma=False,
    )
```

```python
import jax
import jax.numpy as jnp
from jax import lax
from jax.experimental import pallas as pl
from jax.experimental.pallas import tpu as pltpu
from jax.sharding import PartitionSpec as P

ITERS = 4
SIDES = (-1, 0, 1)
TINY = 1e-30
OFF = 2.0

RIM = 4
PAD = 8
HIGH = 32 + 2 * RIM
PITCH = 64 + 2 * PAD
BANDS = 3
LANE_PITCH = 40
HALO = 40
WIDTH = 32 + RIM
FIELD_ROWS = 32 * LANE_PITCH + 16
SUP_PITCH = 48
BLOCK_ROWS = 36 * 8

f32 = jnp.float32


def groups_of(rows):
    third = -(-rows // 24) * 8
    return [(g, g * third, min(third, rows - g * third)) for g in range(3)]


def pack_kernel(perm_ref, sup_ref, up_ref, down_ref):
    rows = perm_ref.shape[0]
    parts = groups_of(rows)
    third = parts[0][2]
    lane = lax.broadcasted_iota(jnp.int32, (third, 128), 1)
    up = down = None
    for g, start, count in parts:
        part = perm_ref[start : start + count, :]
        if count < third:
            part = jnp.concatenate([part, jnp.zeros((third - count, 128), f32)], axis=0)
        high = pltpu.roll(part, WIDTH * (g + 1), 1)
        low = part if g == 0 else pltpu.roll(part, WIDTH * g, 1)
        up = high if up is None else jnp.where(lane < WIDTH * g, up, high)
        down = low if down is None else jnp.where(lane < WIDTH * g, down, low)
    up_ref[:third, :] = up
    down_ref[:third, :] = down
    blocks = sup_ref.shape[0]
    pad = jnp.zeros((blocks, 92), f32)
    wide = [
        jnp.concatenate([sup_ref[:, q, :].astype(f32), pad], axis=1) for q in range(4)
    ]
    up_ref[third:, :] = wide[1] + pltpu.roll(wide[2], 36, 1) + pltpu.roll(wide[3], 72, 1)
    down_ref[third:, :] = wide[0] + pltpu.roll(wide[1], 36, 1) + pltpu.roll(wide[2], 72, 1)


def pack(perm, support):
    third = groups_of(perm.shape[0])[0][2]
    shape = jax.ShapeDtypeStruct((third + support.shape[0], 128), f32)
    return pl.pallas_call(pack_kernel, out_shape=(shape, shape), name="pack")(perm, support)


def widen_kernel(perm_ref, sup_ref, left_ref, right_ref, field_ref, wide_ref, up_ref, down_ref):
    rows = perm_ref.shape[0]
    for g, start, count in groups_of(rows):
        lane = lax.broadcasted_iota(jnp.int32, (count, 128), 1)
        own = perm_ref[start : start + count, :]
        moved = pltpu.roll(own, WIDTH, 1)
        left, right = left_ref[:count, :], right_ref[:count, :]
        if g > 0:
            left = pltpu.roll(left, 128 - WIDTH * g, 1)
        if g != 1:
            right = pltpu.roll(right, (128 + WIDTH - WIDTH * g) % 128, 1)
        field_ref[0, start : start + count, :] = jnp.where(lane < WIDTH, left, moved)
        field_ref[1, start : start + count, :] = pltpu.roll(own, 128 - (64 - WIDTH), 1)
        field_ref[2, start : start + count, :] = jnp.where(
            lane < WIDTH, moved, jnp.where(lane < 2 * WIDTH, right, 0.0)
        )
    for place, band in enumerate((0, 2)):
        up_ref[place * HALO : (place + 1) * HALO, :] = field_ref[band, rows - HALO :, :]
        down_ref[place * HALO : (place + 1) * HALO, :] = field_ref[band, :HALO, :]
    blocks = sup_ref.shape[0]
    third = groups_of(rows)[0][2]
    keep = lax.broadcasted_iota(jnp.int32, (blocks, 128), 1) < 36
    pad = jnp.zeros((blocks, 92), f32)
    for q in range(3):
        for source, place in ((left_ref, q), (right_ref, q + 7)):
            moved = source[third:, :] if q == 0 else pltpu.roll(source[third:, :], 128 - 36 * q, 1)
            wide_ref[place] = jnp.where(keep, moved, 0.0)
    for q in range(4):
        wide_ref[q + 3] = jnp.concatenate([sup_ref[:, q, :].astype(f32), pad], axis=1)
    for q in range(10):
        at = 2 * HALO + 4 * q
        up_ref[at : at + 4, :] = wide_ref[q, blocks - 4 :, :]
        down_ref[at : at + 4, :] = wide_ref[q, :4, :]


def widen(perm, support, from_left, from_right):
    rows, blocks = perm.shape[0], support.shape[0]
    edge = jax.ShapeDtypeStruct((2 * HALO + 40, 128), f32)
    return pl.pallas_call(
        widen_kernel,
        out_shape=(
            jax.ShapeDtypeStruct((BANDS, rows, 128), f32),
            jax.ShapeDtypeStruct((10, blocks, 128), f32),
            edge,
            edge,
        ),
        name="widen",
    )(perm, support, from_left, from_right)


def build_cells(field, cells):
    blank = jnp.zeros((128 - BANDS * LANE_PITCH, 128), f32)
    edge = jnp.zeros((PAD - RIM, 128), f32)

    def row(x, carry):
        parts = [
            field[pl.ds(band * FIELD_ROWS + 256 * m + x + HALO - WIDTH, 8, stride=32), :]
            for band in range(BANDS)
            for m in range(LANE_PITCH // 8)
        ]
        turned = jnp.concatenate(parts + [blank], axis=0).T
        cells[x, 0 : PAD - RIM, :] = edge
        cells[x, PAD - RIM : PITCH - PAD + RIM, :] = turned[: 64 + 2 * RIM]
        cells[x, PITCH - PAD + RIM : PITCH, :] = edge
        return carry

    lax.fori_loop(0, HIGH, row, 0)


PIECES = (
    (PAD - RIM, RIM, 0, 1),
    (PAD, 16, 1, 0),
    (PAD + 16, 16, 1, 1),
    (PAD + 32, 16, 2, 0),
    (PAD + 48, 16, 2, 1),
    (PAD + 64, RIM, 3, 0),
)


def side_of(label, region):
    return (label - region + 1) % 3 - 1


def build_masks(cells, sup, turned, mask):
    blank = jnp.zeros((128 - BANDS * LANE_PITCH, 128), f32)
    for ex in range(5):
        for ey in range(6):
            parts = [
                sup[(2 * band + ey) * SUP_PITCH + ex : (2 * band + ey) * SUP_PITCH + ex + LANE_PITCH, :]
                for band in range(BANDS)
            ]
            turned[ex, ey] = jnp.concatenate(parts + [blank], axis=0).T[:40]
    for tile, (x, rx, tr) in enumerate(
        ((RIM - 1, 0, 1), (RIM, 1, 0), (RIM + 16, 1, 1), (RIM + 32, 2, 0))
    ):
        for start, count, region, tc in PIECES:
            inside = cells[x, start : start + 1, :] > 0.0
            for dx in SIDES:
                for label in range(3):
                    dy = side_of(label, region)
                    if dx == 0 and dy == 0:
                        on = inside
                    else:
                        t = 6 * (2 * (1 - dx) + tr) + 2 * (1 - dy) + tc
                        on = inside & (turned[rx + dx + 1, region + dy + 1, t : t + 1, :] == 1.0)
                    mask[tile, 3 * (dx + 1) + label, start : start + count, :] = jnp.broadcast_to(
                        jnp.where(on, f32(1.0), f32(0.0)), (count, 128)
                    )


def build_faces(cells, coef, values):
    starts = [PAD - RIM + 8 * m for m in range(9)]
    zero = jnp.zeros((8, 128), f32)
    sub = lax.broadcasted_iota(jnp.int32, (8, 128), 0)

    def face(p, q):
        return 2.0 * p * q / jnp.maximum(p + q, TINY)

    def row(x, west):
        east, south = [], []
        for z in starts:
            here = cells[x, z : z + 8, :]
            east.append(face(here, cells[x + 1, z : z + 8, :]))
            south.append(face(here, cells[x, z - 1 : z + 7, :]))
        for m, z in enumerate(starts):
            after = south[m + 1] if m < 8 else zero
            north = jnp.where(sub == 7, pltpu.roll(after, 7, 0), pltpu.roll(south[m], 7, 0))
            scale = OFF / jnp.maximum(west[m] + east[m] + south[m] + north, TINY)
            coef[0, x, z : z + 8, :] = scale * west[m]
            coef[1, x, z : z + 8, :] = scale * east[m]
            coef[2, x, z : z + 8, :] = scale * south[m]
            coef[3, x, z : z + 8, :] = scale * north
        return tuple(east)

    first = tuple(face(cells[0, z : z + 8, :], cells[1, z : z + 8, :]) for z in starts)
    lax.fori_loop(1, HIGH - 1, row, first)

    def begin(x, carry):
        for dx in SIDES:
            for label in range(3):
                for start, count, region, tc in PIECES:
                    own = dx == 0 and side_of(label, region) == 0
                    inside = cells[x, start : start + count, :] > 0.0
                    values[3 * (dx + 1) + label, x, start : start + count, :] = (
                        jnp.where(inside, f32(1.0), f32(0.0)) if own else jnp.zeros((count, 128), f32)
                    )
        return carry

    lax.fori_loop(0, HIGH, begin, 0)


def cut(field, z, edge):
    if not z <= edge < z + 8:
        return field
    sub = lax.broadcasted_iota(jnp.int32, (8, 128), 0)
    return jnp.where(sub == edge - z, 0.0, field)


def smooth_row(old, new, coef, mask, x, tile, starts, first_row, last_row):
    for z in starts:
        rows = slice(z, z + 8)
        west, east = coef[0, x, rows, :], coef[1, x, rows, :]
        south, north = coef[2, x, rows, :], coef[3, x, rows, :]
        edges = (PAD + 32, PAD + 64, PAD)
        souths = [cut(south, z, edge) for edge in edges]
        norths = [cut(north, z, edge - 1) for edge in edges]
        smoothed = []
        total = None
        for dx in SIDES:
            for label in range(3):
                at = 3 * (dx + 1) + label
                term = old[at, x, rows, :]
                if not first_row:
                    term = term + west * old[at, x - 1, rows, :]
                elif dx < 1:
                    term = term + west * old[at + 3, x - 1, rows, :]
                if not last_row:
                    term = term + east * old[at, x + 1, rows, :]
                elif dx > -1:
                    term = term + east * old[at - 3, x + 1, rows, :]
                term = term + souths[label] * old[at, x, z - 1 : z + 7, :]
                term = term + norths[label] * old[at, x, z + 1 : z + 9, :]
                term = mask[tile, at, rows, :] * term
                smoothed.append(term)
                total = term if total is None else total + term
        inverse = 1.0 / jnp.maximum(total, TINY)
        for at in range(9):
            new[at, x, rows, :] = smoothed[at] * inverse


def iterate(old, new, coef, mask, rim):
    if rim:
        starts = [PAD - RIM + 8 * m for m in range(9)]
    else:
        starts = [PAD + 8 * m for m in range(8)]

    def rows(begin, end, tile, first_row=False, last_row=False):
        if end - begin > 1:

            def step(x, carry):
                smooth_row(old, new, coef, mask, x, tile, starts, False, False)
                return carry

            lax.fori_loop(begin, end, step, 0)
        elif end > begin:
            smooth_row(old, new, coef, mask, begin, tile, starts, first_row, last_row)

    rows(RIM - rim, RIM - 1, 0)
    if rim:
        rows(RIM - 1, RIM, 0, last_row=True)
    rows(RIM, RIM + 1, 1, first_row=True)

    def inner(x, carry):
        tile = jnp.where(x < RIM + 16, 1, 2)
        smooth_row(old, new, coef, mask, x, tile, starts, False, False)
        return carry

    lax.fori_loop(RIM + 1, RIM + 31, inner, 0)
    rows(RIM + 31, RIM + 32, 2, last_row=True)
    if rim:
        rows(RIM + 32, RIM + 33, 3, first_row=True)
    rows(RIM + 33, RIM + 32 + rim, 3)


def to_tiles(values, out):
    def half_tile(part, carry):
        for dx in SIDES:
            for label in range(3):
                for tc in range(4):
                    z = PAD + 16 * tc
                    region = 1 + tc // 2
                    dy = side_of(label, region)
                    cells = [
                        values[3 * (dx + 1) + label, RIM + 8 * part + u, z : z + 16, :]
                        for u in range(8)
                    ]
                    turned = jnp.concatenate(cells, axis=0).T
                    t = 12 * (1 - dx) + 2 * (1 - dy) + tc % 2
                    for band in range(BANDS):
                        q = 2 * band - 2 + region + dy
                        if 0 <= q < 4:
                            for m in range(LANE_PITCH // 8):
                                row = (8 * m + 1 + dx) * BLOCK_ROWS + 8 * t + q
                                out[
                                    pl.ds(row + (part // 2) * 48 + (part % 2) * 4, 8, stride=BLOCK_ROWS), :
                                ] = turned[LANE_PITCH * band + 8 * m : LANE_PITCH * band + 8 * m + 8]
        return carry

    lax.fori_loop(0, 4, half_tile, 0)


def main_kernel(
    field_hbm, sup_ref, low_ref, high_ref, out_hbm,
    field, sup, cells, turned, mask, coef, values, other, out, sem,
):
    rows = field_hbm.shape[1]
    blocks = sup_ref.shape[1]
    copies = []
    for band in range(BANDS):
        copy = pltpu.make_async_copy(
            field_hbm.at[band],
            field.at[pl.ds(band * FIELD_ROWS + HALO, rows), :],
            sem.at[band],
        )
        copy.start()
        copies.append(copy)
    lane = lax.broadcasted_iota(jnp.int32, (HALO, 128), 1)
    for ref, at in ((low_ref, 0), (high_ref, HALO + rows)):
        left, right = ref[:HALO, :], ref[HALO : 2 * HALO, :]
        field[at : at + HALO, :] = left
        at = at + FIELD_ROWS
        field[at : at + HALO, :] = jnp.where(lane < 64, pltpu.roll(left, 64, 1), pltpu.roll(right, 64, 1))
        at = at + FIELD_ROWS
        field[at : at + HALO, :] = right
    rest = FIELD_ROWS - rows - 2 * HALO
    for band in range(BANDS):
        at = band * FIELD_ROWS + rows + 2 * HALO
        field[at : at + rest, :] = jnp.zeros((rest, 128), f32)
    for q in range(10):
        at = q * SUP_PITCH
        sup[at : at + 3, :] = low_ref[2 * HALO + 4 * q + 1 : 2 * HALO + 4 * q + 4, :]
        sup[at + 3 : at + 3 + blocks, :] = sup_ref[q]
        sup[at + 3 + blocks : at + 6 + blocks, :] = high_ref[2 * HALO + 4 * q : 2 * HALO + 4 * q + 3, :]
        sup[at + 6 + blocks : at + SUP_PITCH, :] = jnp.zeros((SUP_PITCH - 6 - blocks, 128), f32)
    for copy in copies:
        copy.wait()
    build_cells(field, cells)
    build_masks(cells, sup, turned, mask)
    build_faces(cells, coef, values)
    for count in range(ITERS):
        old, new = (values, other) if count % 2 == 0 else (other, values)
        iterate(old, new, coef, mask, ITERS - 1 - count)
    to_tiles(values if ITERS % 2 == 0 else other, out)
    copy = pltpu.make_async_copy(
        out.at[pl.ds(2 * BLOCK_ROWS, blocks * BLOCK_ROWS), :], out_hbm, sem.at[0]
    )
    copy.start()
    copy.wait()


def smooth(field, sup, low, high):
    blocks = sup.shape[1]
    vmem = pl.BlockSpec(memory_space=pltpu.VMEM)
    hbm = pl.BlockSpec(memory_space=pl.ANY)
    return pl.pallas_call(
        main_kernel,
        out_shape=jax.ShapeDtypeStruct((blocks * BLOCK_ROWS, 128), f32),
        in_specs=[hbm, vmem, vmem, vmem],
        out_specs=hbm,
        scratch_shapes=[
            pltpu.VMEM((BANDS * FIELD_ROWS, 128), f32),
            pltpu.VMEM((10 * SUP_PITCH, 128), f32),
            pltpu.VMEM((HIGH, PITCH, 128), f32),
            pltpu.VMEM((5, 6, 40, 128), f32),
            pltpu.VMEM((4, 9, PITCH, 128), f32),
            pltpu.VMEM((4, HIGH, PITCH, 128), f32),
            pltpu.VMEM((9, HIGH, PITCH, 128), f32),
            pltpu.VMEM((9, HIGH, PITCH, 128), f32),
            pltpu.VMEM(((LANE_PITCH + 2) * BLOCK_ROWS, 128), f32),
            pltpu.SemaphoreType.DMA((BANDS,)),
        ],
        compiler_params=pltpu.CompilerParams(vmem_limit_bytes=60 * 1024 * 1024),
        name="smooth",
    )(field, sup, low, high)


def neighbours(up, down, axis):
    count = lax.axis_size(axis)
    forward = [(i, i + 1) for i in range(count - 1)]
    backward = [(i + 1, i) for i in range(count - 1)]
    return lax.ppermute(up, axis, forward), lax.ppermute(down, axis, backward)


def body(permeability, support):
    up, down = pack(permeability, support)
    from_left, from_right = neighbours(up, down, "gy")
    field, sup, up, down = widen(permeability, support, from_left, from_right)
    low, high = neighbours(up, down, "gx")
    tiles = smooth(field, sup, low, high).reshape(support.shape[0], 36, 2, 4, 128)
    return tiles.transpose(0, 3, 1, 2, 4).reshape(support.shape + (256,))


def solution(mesh):
    return jax.shard_map(
        body,
        mesh=mesh,
        in_specs=(P(("grp", "gx"), "gy"), P(("grp", "gx"), "gy", None)),
        out_specs=P(("grp", "gx"), "gy", None, None),
        check_vma=False,
    )
```

```python
import functools

import jax
import jax.numpy as jnp
from jax import lax
from jax.experimental import pallas as pl
from jax.experimental.pallas import tpu as pltpu
from jax.sharding import PartitionSpec as P

ITERS = 4
SIDES = (-1, 0, 1)
TINY = 1e-30
OFF = 2.0

RIM = 4
PAD = 8
HIGH = 32 + 2 * RIM
PITCH = 64 + 2 * PAD
BANDS = 3
LANE_PITCH = 40
HALO = 40
WIDTH = 32 + RIM
FIELD_ROWS = 32 * LANE_PITCH + 16
SUP_PITCH = 48
BLOCK_ROWS = 36 * 8

f32 = jnp.float32


def cost(amount):
    return pl.CostEstimate(flops=amount, bytes_accessed=amount, transcendentals=0)


def support_rows(sup_ref):
    pad = jnp.zeros((sup_ref.shape[0], 92), f32)
    return [jnp.concatenate([sup_ref[:, q, :].astype(f32), pad], axis=1) for q in range(4)]


def groups_of(rows):
    third = -(-rows // 24) * 8
    return [(g, g * third, min(third, rows - g * third)) for g in range(3)]


def pack_kernel(perm_ref, sup_ref, up_ref, down_ref):
    rows = perm_ref.shape[0]
    parts = groups_of(rows)
    third = parts[0][2]
    lane = lax.broadcasted_iota(jnp.int32, (third, 128), 1)
    up = down = None
    for g, start, count in parts:
        part = perm_ref[start : start + count, :]
        if count < third:
            part = jnp.concatenate([part, jnp.zeros((third - count, 128), f32)], axis=0)
        high = pltpu.roll(part, WIDTH * (g + 1), 1)
        low = part if g == 0 else pltpu.roll(part, WIDTH * g, 1)
        up = high if up is None else jnp.where(lane < WIDTH * g, up, high)
        down = low if down is None else jnp.where(lane < WIDTH * g, down, low)
    up_ref[:third, :] = up
    down_ref[:third, :] = down
    wide = support_rows(sup_ref)
    up_ref[third:, :] = wide[1] + pltpu.roll(wide[2], 36, 1) + pltpu.roll(wide[3], 72, 1)
    down_ref[third:, :] = wide[0] + pltpu.roll(wide[1], 36, 1) + pltpu.roll(wide[2], 72, 1)


def pack(perm, support):
    third = groups_of(perm.shape[0])[0][2]
    shape = jax.ShapeDtypeStruct((third + support.shape[0], 128), f32)
    return pl.pallas_call(pack_kernel, out_shape=(shape, shape), name="pack")(perm, support)


def bands_of(own, left, right, g):
    lane = lax.broadcasted_iota(jnp.int32, own.shape, 1)
    moved = pltpu.roll(own, WIDTH, 1)
    if g > 0:
        left = pltpu.roll(left, 128 - WIDTH * g, 1)
    if g != 1:
        right = pltpu.roll(right, (128 + WIDTH - WIDTH * g) % 128, 1)
    return (
        jnp.where(lane < WIDTH, left, moved),
        pltpu.roll(own, 64 + WIDTH, 1),
        jnp.where(lane < WIDTH, moved, jnp.where(lane < 2 * WIDTH, right, 0.0)),
    )


def wide_support(sup_ref, left, right):
    shift = [0, 128 - 36, 128 - 72]
    low = [pltpu.roll(left, by, 1) if by else left for by in shift]
    high = [pltpu.roll(right, by, 1) if by else right for by in shift]
    return low + support_rows(sup_ref) + high


def edge_kernel(perm_ref, sup_ref, left_ref, right_ref, up_ref, down_ref):
    rows, blocks = perm_ref.shape[0], sup_ref.shape[0]
    groups = groups_of(rows)
    third = groups[0][2]
    for ref, g, start, block in ((up_ref, 2, rows - HALO, blocks - 4), (down_ref, 0, 0, 0)):
        packed = slice(start - groups[g][1], start - groups[g][1] + HALO)
        bands = bands_of(perm_ref[start : start + HALO, :], left_ref[packed, :], right_ref[packed, :], g)
        ref[:HALO, :] = bands[0]
        ref[HALO : 2 * HALO, :] = bands[2]
        four = slice(third + block, third + block + 4)
        wide = wide_support(sup_ref.at[pl.ds(block, 4)], left_ref[four, :], right_ref[four, :])
        for q in range(10):
            ref[2 * HALO + 4 * q : 2 * HALO + 4 * q + 4, :] = wide[q]


def edges(perm, support, from_left, from_right):
    edge = jax.ShapeDtypeStruct((2 * HALO + 40, 128), f32)
    return pl.pallas_call(
        edge_kernel, out_shape=(edge, edge), cost_estimate=cost(100_000), name="edges"
    )(perm, support, from_left, from_right)


def widen_kernel(perm_ref, sup_ref, left_ref, right_ref, field_ref, wide_ref):
    rows = perm_ref.shape[0]
    groups = groups_of(rows)
    third = groups[0][2]
    for g, start, count in groups:
        bands = bands_of(
            perm_ref[start : start + count, :], left_ref[:count, :], right_ref[:count, :], g
        )
        for band in range(BANDS):
            field_ref[band, start : start + count, :] = bands[band]
    for q, wide in enumerate(wide_support(sup_ref, left_ref[third:, :], right_ref[third:, :])):
        wide_ref[q] = wide


def widen(perm, support, from_left, from_right):
    rows, blocks = perm.shape[0], support.shape[0]
    return pl.pallas_call(
        widen_kernel,
        out_shape=(
            jax.ShapeDtypeStruct((BANDS, rows, 128), f32),
            jax.ShapeDtypeStruct((10, blocks, 128), f32),
        ),
        cost_estimate=cost(4_000_000),
        name="widen",
    )(perm, support, from_left, from_right)


def build_cells(field, cells):
    blank = jnp.zeros((128 - BANDS * LANE_PITCH, 128), f32)
    edge = jnp.zeros((PAD - RIM, 128), f32)

    def row(step, carry):
        for u in range(10):
            x = 10 * step + u
            parts = [
                field[pl.ds(band * FIELD_ROWS + 256 * m + x + HALO - WIDTH, 8, stride=32), :]
                for band in range(BANDS)
                for m in range(LANE_PITCH // 8)
            ]
            turned = jnp.concatenate(parts + [blank], axis=0).T
            cells[x, 0 : PAD - RIM, :] = edge
            cells[x, PAD - RIM : PITCH - PAD + RIM, :] = turned[: 64 + 2 * RIM]
            cells[x, PITCH - PAD + RIM : PITCH, :] = edge
        return carry

    lax.fori_loop(0, HIGH // 10, row, 0)


PIECES = (
    (PAD - RIM, RIM, 0, 1),
    (PAD, 16, 1, 0),
    (PAD + 16, 16, 1, 1),
    (PAD + 32, 16, 2, 0),
    (PAD + 48, 16, 2, 1),
    (PAD + 64, RIM, 3, 0),
)


def side_of(label, region):
    return (label - region + 1) % 3 - 1


def build_masks(cells, sup, turned, mask):
    blank = jnp.zeros((128 - BANDS * LANE_PITCH, 128), f32)
    for ex in range(5):
        for ey in range(6):
            parts = [
                sup[(2 * band + ey) * SUP_PITCH + ex : (2 * band + ey) * SUP_PITCH + ex + LANE_PITCH, :]
                for band in range(BANDS)
            ]
            turned[ex, ey] = jnp.concatenate(parts + [blank], axis=0).T[:40]
    for tile, (x, rx, tr) in enumerate(
        ((RIM - 1, 0, 1), (RIM, 1, 0), (RIM + 16, 1, 1), (RIM + 32, 2, 0))
    ):
        for start, count, region, tc in PIECES:
            inside = cells[x, start : start + 1, :] > 0.0
            for dx in SIDES:
                for label in range(3):
                    dy = side_of(label, region)
                    if dx == 0 and dy == 0:
                        on = inside
                    else:
                        t = 6 * (2 * (1 - dx) + tr) + 2 * (1 - dy) + tc
                        on = inside & (turned[rx + dx + 1, region + dy + 1, t : t + 1, :] == 1.0)
                    mask[tile, 3 * (dx + 1) + label, start : start + count, :] = jnp.broadcast_to(
                        jnp.where(on, f32(1.0), f32(0.0)), (count, 128)
                    )


def build_faces(cells, coef):
    starts = [PAD - RIM + 8 * m for m in range(9)]
    zero = jnp.zeros((8, 128), f32)
    sub = lax.broadcasted_iota(jnp.int32, (8, 128), 0)

    def face(p, q):
        return 2.0 * p * q / jnp.maximum(p + q, TINY)

    def row(x, west):
        east, south = [], []
        for z in starts:
            here = cells[x, z : z + 8, :]
            east.append(face(here, cells[x + 1, z : z + 8, :]))
            south.append(face(here, cells[x, z - 1 : z + 7, :]))
        for m, z in enumerate(starts):
            after = south[m + 1] if m < 8 else zero
            north = jnp.where(sub == 7, pltpu.roll(after, 7, 0), pltpu.roll(south[m], 7, 0))
            scale = OFF / jnp.maximum(west[m] + east[m] + south[m] + north, TINY)
            coef[0, x, z : z + 8, :] = scale * west[m]
            coef[1, x, z : z + 8, :] = scale * east[m]
            coef[2, x, z : z + 8, :] = scale * south[m]
            coef[3, x, z : z + 8, :] = scale * north
        return tuple(east)

    first = tuple(face(cells[0, z : z + 8, :], cells[1, z : z + 8, :]) for z in starts)
    lax.fori_loop(1, HIGH - 1, row, first)


def cut(field, z, edge):
    if not z <= edge < z + 8:
        return field
    sub = lax.broadcasted_iota(jnp.int32, (8, 128), 0)
    return jnp.where(sub == edge - z, 0.0, field)


EDGES = (PAD + 32, PAD + 64, PAD)


def region_of(z):
    return 0 if z < PAD else 3 if z >= PAD + 64 else 1 + (z - PAD) // 32


def finish(terms, new, mask, x, tile, rows):
    total = None
    for at, term in enumerate(terms):
        if term is not None:
            terms[at] = term = mask[tile, at, rows, :] * term
            total = term if total is None else total + term
    inverse = 1.0 / jnp.maximum(total, TINY)
    for at, term in enumerate(terms):
        new[at, x, rows, :] = jnp.zeros((8, 128), f32) if term is None else term * inverse


def where_own(label, z, value):
    own = [side_of(label, region_of(z + i)) == 0 for i in range(8)]
    if all(own):
        return value
    if not any(own):
        return None
    sub = lax.broadcasted_iota(jnp.int32, (8, 128), 0)
    first, count = own.index(True), sum(own)
    return jnp.where((sub >= first) & (sub < first + count), value, 0.0)


def add(a, b):
    return b if a is None else a if b is None else a + b


def first_vector(new, coef, mask, x, tile, z, first_row, last_row):
    rows = slice(z, z + 8)
    west, east = coef[0, x, rows, :], coef[1, x, rows, :]
    south, north = coef[2, x, rows, :], coef[3, x, rows, :]
    middle = jnp.ones((8, 128), f32)
    middle = middle if first_row else middle + west
    middle = middle if last_row else middle + east
    terms = [None] * 9
    for label in range(3):
        term = where_own(label, z, middle)
        term = add(term, where_own(label, z - 1, cut(south, z, EDGES[label])))
        terms[3 + label] = add(term, where_own(label, z + 1, cut(north, z, EDGES[label] - 1)))
        if first_row:
            terms[label] = where_own(label, z, west)
        if last_row:
            terms[6 + label] = where_own(label, z, east)
    finish(terms, new, mask, x, tile, rows)


def smooth_vector(old, new, coef, mask, x, tile, z, first_row, last_row):
    rows = slice(z, z + 8)
    west, east = coef[0, x, rows, :], coef[1, x, rows, :]
    south, north = coef[2, x, rows, :], coef[3, x, rows, :]
    souths = [cut(south, z, edge) for edge in EDGES]
    norths = [cut(north, z, edge - 1) for edge in EDGES]
    terms = []
    for dx in SIDES:
        for label in range(3):
            at = 3 * (dx + 1) + label
            term = old[at, x, rows, :]
            if not first_row:
                term = term + west * old[at, x - 1, rows, :]
            elif dx < 1:
                term = term + west * old[at + 3, x - 1, rows, :]
            if not last_row:
                term = term + east * old[at, x + 1, rows, :]
            elif dx > -1:
                term = term + east * old[at - 3, x + 1, rows, :]
            term = term + souths[label] * old[at, x, z - 1 : z + 7, :]
            term = term + norths[label] * old[at, x, z + 1 : z + 9, :]
            terms.append(term)
    finish(terms, new, mask, x, tile, rows)


def iterate(vector, rim):
    def row(x, tile, first_row=False, last_row=False):
        for m in range(9):
            vector(x, tile, PAD - RIM + 8 * m, first_row, last_row)

    def rows(begin, end, tile):
        def step(x, carry):
            row(x, tile)
            return carry

        lax.fori_loop(begin, end, step, 0)

    rows(RIM - rim, RIM - 1, 0)
    row(RIM - 1, 0, last_row=True)
    row(RIM, 1, first_row=True)

    def inner(x, carry):
        row(x, jnp.where(x < RIM + 16, 1, 2))
        return carry

    lax.fori_loop(RIM + 1, RIM + 31, inner, 0)
    row(RIM + 31, 2, last_row=True)
    row(RIM + 32, 3, first_row=True)
    rows(RIM + 33, RIM + 32 + rim, 3)


def turn_tile(values, staged, part, dx, label, tc):
    z = PAD + 16 * tc
    region = 1 + tc // 2
    dy = side_of(label, region)
    cells = [values[3 * (dx + 1) + label, RIM + 8 * part + u, z : z + 16, :] for u in range(8)]
    turned = jnp.concatenate(cells, axis=0).T
    t = 6 * (2 * (1 - dx) + part // 2) + 2 * (1 - dy) + tc % 2
    for band in range(BANDS):
        q = 2 * band - 2 + region + dy
        if 0 <= q < 4:
            at = (8 * t + 4 * (part % 2) + q) * LANE_PITCH
            staged[at : at + LANE_PITCH, :] = turned[LANE_PITCH * band : LANE_PITCH * (band + 1)]


def gather_tiles(staged, out, blocks, tr):
    def block(p, carry):
        for side in range(3):
            for b in range(6):
                t = 6 * (2 * side + tr) + b
                out[p, side, tr, 8 * b : 8 * b + 8, :] = staged[
                    pl.ds(8 * t * LANE_PITCH + p + side, 8, stride=LANE_PITCH), :
                ]
        return carry

    lax.fori_loop(0, blocks, block, 0)


def last_iteration(old, new, coef, mask, staged, out, out_hbm, sem, blocks):
    jobs = [(dx, label, tc) for dx in SIDES for label in range(3) for tc in range(4)]
    copies = []
    for part in range(5):
        if part < 4:
            for u in range(8):
                x = RIM + 8 * part + u
                for m in range(8):
                    smooth_vector(
                        old, new, coef, mask, x, 1 + part // 2, PAD + 8 * m, x == RIM, x == RIM + 31
                    )
                if part > 0:
                    for job in jobs[36 * u // 8 : 36 * (u + 1) // 8]:
                        turn_tile(new, staged, part - 1, *job)
        else:
            for job in jobs:
                turn_tile(new, staged, part - 1, *job)
        if part in (2, 4):
            tr = part // 2 - 1
            gather_tiles(staged, out, blocks, tr)
            copy = pltpu.make_async_copy(out.at[:, :, tr], out_hbm.at[:, :, tr], sem.at[tr])
            copy.start()
            copies.append(copy)
    for copy in copies:
        copy.wait()


def main_kernel(
    field_hbm, sup_ref, low_ref, high_ref, out_hbm,
    field, sup, cells, turned, mask, coef, values, other, staged, out, sem,
):
    rows = field_hbm.shape[1]
    blocks = sup_ref.shape[1]
    copies = []
    for band in range(BANDS):
        copy = pltpu.make_async_copy(
            field_hbm.at[band],
            field.at[pl.ds(band * FIELD_ROWS + HALO, rows), :],
            sem.at[band],
        )
        copy.start()
        copies.append(copy)
    lane = lax.broadcasted_iota(jnp.int32, (HALO, 128), 1)
    for ref, at in ((low_ref, 0), (high_ref, HALO + rows)):
        left, right = ref[:HALO, :], ref[HALO : 2 * HALO, :]
        field[at : at + HALO, :] = left
        at = at + FIELD_ROWS
        field[at : at + HALO, :] = jnp.where(lane < 64, pltpu.roll(left, 64, 1), pltpu.roll(right, 64, 1))
        at = at + FIELD_ROWS
        field[at : at + HALO, :] = right
    rest = FIELD_ROWS - rows - 2 * HALO
    for band in range(BANDS):
        at = band * FIELD_ROWS + rows + 2 * HALO
        field[at : at + rest, :] = jnp.zeros((rest, 128), f32)
    for q in range(10):
        at = q * SUP_PITCH
        sup[at : at + 3, :] = low_ref[2 * HALO + 4 * q + 1 : 2 * HALO + 4 * q + 4, :]
        sup[at + 3 : at + 3 + blocks, :] = sup_ref[q]
        sup[at + 3 + blocks : at + 6 + blocks, :] = high_ref[2 * HALO + 4 * q : 2 * HALO + 4 * q + 3, :]
        sup[at + 6 + blocks : at + SUP_PITCH, :] = jnp.zeros((SUP_PITCH - 6 - blocks, 128), f32)
    for copy in copies:
        copy.wait()
    build_cells(field, cells)
    build_masks(cells, sup, turned, mask)
    build_faces(cells, coef)
    iterate(functools.partial(first_vector, other, coef, mask), ITERS - 1)
    old, new = other, values
    for count in range(1, ITERS - 1):
        iterate(functools.partial(smooth_vector, old, new, coef, mask), ITERS - 1 - count)
        old, new = new, old
    last_iteration(old, new, coef, mask, staged, out, out_hbm, sem, blocks)


def smooth(field, sup, low, high):
    blocks = sup.shape[1]
    vmem = pl.BlockSpec(memory_space=pltpu.VMEM)
    hbm = pl.BlockSpec(memory_space=pl.ANY)
    return pl.pallas_call(
        main_kernel,
        out_shape=jax.ShapeDtypeStruct((blocks, 3, 2, 48, 128), f32),
        in_specs=[hbm, vmem, vmem, vmem],
        out_specs=hbm,
        scratch_shapes=[
            pltpu.VMEM((BANDS * FIELD_ROWS, 128), f32),
            pltpu.VMEM((10 * SUP_PITCH, 128), f32),
            pltpu.VMEM((HIGH, PITCH, 128), f32),
            pltpu.VMEM((5, 6, 40, 128), f32),
            pltpu.VMEM((4, 9, PITCH, 128), f32),
            pltpu.VMEM((4, HIGH, PITCH, 128), f32),
            pltpu.VMEM((9, HIGH, PITCH, 128), f32),
            pltpu.VMEM((9, HIGH, PITCH, 128), f32),
            pltpu.VMEM((LANE_PITCH * BLOCK_ROWS, 128), f32),
            pltpu.VMEM((blocks, 3, 2, 48, 128), f32),
            pltpu.SemaphoreType.DMA((BANDS,)),
        ],
        compiler_params=pltpu.CompilerParams(vmem_limit_bytes=60 * 1024 * 1024),
        name="smooth",
    )(field, sup, low, high)


def neighbours(up, down, axis):
    count = lax.axis_size(axis)
    forward = [(i, i + 1) for i in range(count - 1)]
    backward = [(i + 1, i) for i in range(count - 1)]
    return lax.ppermute(up, axis, forward), lax.ppermute(down, axis, backward)


def body(permeability, support):
    up, down = pack(permeability, support)
    from_left, from_right = neighbours(up, down, "gy")
    up, down = edges(permeability, support, from_left, from_right)
    low, high = neighbours(up, down, "gx")
    field, sup = widen(permeability, support, from_left, from_right)
    tiles = smooth(field, sup, low, high).reshape(support.shape[0], 36, 2, 4, 128)
    return tiles.transpose(0, 3, 1, 2, 4).reshape(support.shape + (256,))


def solution(mesh):
    return jax.shard_map(
        body,
        mesh=mesh,
        in_specs=(P(("grp", "gx"), "gy"), P(("grp", "gx"), "gy", None)),
        out_specs=P(("grp", "gx"), "gy", None, None),
        check_vma=False,
    )
```

```python
import functools

import jax
import jax.numpy as jnp
from jax import lax
from jax.experimental import pallas as pl
from jax.experimental.pallas import tpu as pltpu
from jax.sharding import PartitionSpec as P

ITERS = 4
SIDES = (-1, 0, 1)
TINY = 1e-30
OFF = 2.0

RIM = 4
PAD = 8
HIGH = 32 + 2 * RIM
PITCH = 64 + 2 * PAD
BANDS = 3
LANE_PITCH = 40
HALO = 40
WIDTH = 32 + RIM
FIELD_ROWS = 32 * LANE_PITCH + 16
SUP_PITCH = 48
BLOCK_ROWS = 36 * 8

f32 = jnp.float32


def cost(amount):
    return pl.CostEstimate(flops=amount, bytes_accessed=amount, transcendentals=0)


def support_rows(sup_ref):
    pad = jnp.zeros((sup_ref.shape[0], 92), f32)
    return [jnp.concatenate([sup_ref[:, q, :].astype(f32), pad], axis=1) for q in range(4)]


def groups_of(rows):
    third = -(-rows // 24) * 8
    return [(g, g * third, min(third, rows - g * third)) for g in range(3)]


def pack_kernel(perm_ref, sup_ref, up_ref, down_ref):
    rows = perm_ref.shape[0]
    parts = groups_of(rows)
    third = parts[0][2]
    lane = lax.broadcasted_iota(jnp.int32, (third, 128), 1)
    up = down = None
    for g, start, count in parts:
        part = perm_ref[start : start + count, :]
        if count < third:
            part = jnp.concatenate([part, jnp.zeros((third - count, 128), f32)], axis=0)
        high = pltpu.roll(part, WIDTH * (g + 1), 1)
        low = part if g == 0 else pltpu.roll(part, WIDTH * g, 1)
        up = high if up is None else jnp.where(lane < WIDTH * g, up, high)
        down = low if down is None else jnp.where(lane < WIDTH * g, down, low)
    up_ref[:third, :] = up
    down_ref[:third, :] = down
    wide = support_rows(sup_ref)
    up_ref[third:, :] = wide[1] + pltpu.roll(wide[2], 36, 1) + pltpu.roll(wide[3], 72, 1)
    down_ref[third:, :] = wide[0] + pltpu.roll(wide[1], 36, 1) + pltpu.roll(wide[2], 72, 1)


def pack(perm, support):
    third = groups_of(perm.shape[0])[0][2]
    shape = jax.ShapeDtypeStruct((third + support.shape[0], 128), f32)
    return pl.pallas_call(pack_kernel, out_shape=(shape, shape), name="pack")(perm, support)


def bands_of(own, left, right, g):
    lane = lax.broadcasted_iota(jnp.int32, own.shape, 1)
    moved = pltpu.roll(own, WIDTH, 1)
    if g > 0:
        left = pltpu.roll(left, 128 - WIDTH * g, 1)
    if g != 1:
        right = pltpu.roll(right, (128 + WIDTH - WIDTH * g) % 128, 1)
    return (
        jnp.where(lane < WIDTH, left, moved),
        pltpu.roll(own, 64 + WIDTH, 1),
        jnp.where(lane < WIDTH, moved, jnp.where(lane < 2 * WIDTH, right, 0.0)),
    )


def wide_support(sup_ref, left, right):
    shift = [0, 128 - 36, 128 - 72]
    low = [pltpu.roll(left, by, 1) if by else left for by in shift]
    high = [pltpu.roll(right, by, 1) if by else right for by in shift]
    return low + support_rows(sup_ref) + high


def edge_kernel(perm_ref, sup_ref, left_ref, right_ref, up_ref, down_ref):
    rows, blocks = perm_ref.shape[0], sup_ref.shape[0]
    groups = groups_of(rows)
    third = groups[0][2]
    for ref, g, start, block in ((up_ref, 2, rows - HALO, blocks - 4), (down_ref, 0, 0, 0)):
        packed = slice(start - groups[g][1], start - groups[g][1] + HALO)
        bands = bands_of(perm_ref[start : start + HALO, :], left_ref[packed, :], right_ref[packed, :], g)
        ref[:HALO, :] = bands[0]
        ref[HALO : 2 * HALO, :] = bands[2]
        four = slice(third + block, third + block + 4)
        wide = wide_support(sup_ref.at[pl.ds(block, 4)], left_ref[four, :], right_ref[four, :])
        for q in range(10):
            ref[2 * HALO + 4 * q : 2 * HALO + 4 * q + 4, :] = wide[q]


def edges(perm, support, from_left, from_right):
    edge = jax.ShapeDtypeStruct((2 * HALO + 40, 128), f32)
    return pl.pallas_call(
        edge_kernel, out_shape=(edge, edge), cost_estimate=cost(100_000), name="edges"
    )(perm, support, from_left, from_right)


def widen_kernel(perm_ref, sup_ref, left_ref, right_ref, field_ref, wide_ref):
    rows = perm_ref.shape[0]
    groups = groups_of(rows)
    third = groups[0][2]
    for g, start, count in groups:
        bands = bands_of(
            perm_ref[start : start + count, :], left_ref[:count, :], right_ref[:count, :], g
        )
        for band in range(BANDS):
            field_ref[band, start : start + count, :] = bands[band]
    for q, wide in enumerate(wide_support(sup_ref, left_ref[third:, :], right_ref[third:, :])):
        wide_ref[q] = wide


def widen(perm, support, from_left, from_right):
    rows, blocks = perm.shape[0], support.shape[0]
    return pl.pallas_call(
        widen_kernel,
        out_shape=(
            jax.ShapeDtypeStruct((BANDS, rows, 128), f32),
            jax.ShapeDtypeStruct((10, blocks, 128), f32),
        ),
        cost_estimate=cost(4_000_000),
        name="widen",
    )(perm, support, from_left, from_right)


def build_cells(field, cells):
    blank = jnp.zeros((128 - BANDS * LANE_PITCH, 128), f32)
    edge = jnp.zeros((PAD - RIM, 128), f32)

    def row(step, carry):
        for u in range(10):
            x = 10 * step + u
            parts = [
                field[pl.ds(band * FIELD_ROWS + 256 * m + x + HALO - WIDTH, 8, stride=32), :]
                for band in range(BANDS)
                for m in range(LANE_PITCH // 8)
            ]
            turned = jnp.concatenate(parts + [blank], axis=0).T
            cells[x, 0 : PAD - RIM, :] = edge
            cells[x, PAD - RIM : PITCH - PAD + RIM, :] = turned[: 64 + 2 * RIM]
            cells[x, PITCH - PAD + RIM : PITCH, :] = edge
        return carry

    lax.fori_loop(0, HIGH // 10, row, 0)


PIECES = (
    (PAD - RIM, RIM, 0, 1),
    (PAD, 16, 1, 0),
    (PAD + 16, 16, 1, 1),
    (PAD + 32, 16, 2, 0),
    (PAD + 48, 16, 2, 1),
    (PAD + 64, RIM, 3, 0),
)


def side_of(label, region):
    return (label - region + 1) % 3 - 1


def turn_support(sup, turned):
    blank = jnp.zeros((128 - BANDS * LANE_PITCH, 128), f32)
    for ex in range(5):
        for ey in range(6):
            parts = [
                sup[(2 * band + ey) * SUP_PITCH + ex : (2 * band + ey) * SUP_PITCH + ex + LANE_PITCH, :]
                for band in range(BANDS)
            ]
            turned[ex, ey] = jnp.concatenate(parts + [blank], axis=0).T[:40]


def build_masks(cells, turned, mask):
    for tile, (x, rx, tr) in enumerate(
        ((RIM - 1, 0, 1), (RIM, 1, 0), (RIM + 16, 1, 1), (RIM + 32, 2, 0))
    ):
        for start, count, region, tc in PIECES:
            inside = cells[x, start : start + 1, :] > 0.0
            for dx in SIDES:
                for label in range(3):
                    dy = side_of(label, region)
                    if dx == 0 and dy == 0:
                        on = inside
                    else:
                        t = 6 * (2 * (1 - dx) + tr) + 2 * (1 - dy) + tc
                        on = inside & (turned[rx + dx + 1, region + dy + 1, t : t + 1, :] == 1.0)
                    mask[tile, 3 * (dx + 1) + label, start : start + count, :] = jnp.broadcast_to(
                        jnp.where(on, f32(1.0), f32(0.0)), (count, 128)
                    )


def build_faces(cells, coef):
    starts = [PAD - RIM + 8 * m for m in range(9)]
    zero = jnp.zeros((8, 128), f32)
    sub = lax.broadcasted_iota(jnp.int32, (8, 128), 0)

    def face(p, q):
        return 2.0 * p * q / jnp.maximum(p + q, TINY)

    def row(x, west):
        east, south = [], []
        for z in starts:
            here = cells[x, z : z + 8, :]
            east.append(face(here, cells[x + 1, z : z + 8, :]))
            south.append(face(here, cells[x, z - 1 : z + 7, :]))
        for m, z in enumerate(starts):
            after = south[m + 1] if m < 8 else zero
            north = jnp.where(sub == 7, pltpu.roll(after, 7, 0), pltpu.roll(south[m], 7, 0))
            scale = OFF / jnp.maximum(west[m] + east[m] + south[m] + north, TINY)
            coef[0, x, z : z + 8, :] = scale * west[m]
            coef[1, x, z : z + 8, :] = scale * east[m]
            coef[2, x, z : z + 8, :] = scale * south[m]
            coef[3, x, z : z + 8, :] = scale * north
        return tuple(east)

    first = tuple(face(cells[0, z : z + 8, :], cells[1, z : z + 8, :]) for z in starts)
    lax.fori_loop(1, HIGH - 1, row, first)


def cut(field, z, edge):
    if not z <= edge < z + 8:
        return field
    sub = lax.broadcasted_iota(jnp.int32, (8, 128), 0)
    return jnp.where(sub == edge - z, 0.0, field)


EDGES = (PAD + 32, PAD + 64, PAD)


def region_of(z):
    return 0 if z < PAD else 3 if z >= PAD + 64 else 1 + (z - PAD) // 32


def finish(terms, new, mask, x, tile, rows):
    total = None
    for at, term in enumerate(terms):
        if term is not None:
            terms[at] = term = mask[tile, at, rows, :] * term
            total = term if total is None else total + term
    inverse = 1.0 / jnp.maximum(total, TINY)
    for at, term in enumerate(terms):
        new[at, x, rows, :] = jnp.zeros((8, 128), f32) if term is None else term * inverse


def where_own(label, z, value):
    own = [side_of(label, region_of(z + i)) == 0 for i in range(8)]
    if all(own):
        return value
    if not any(own):
        return None
    sub = lax.broadcasted_iota(jnp.int32, (8, 128), 0)
    first, count = own.index(True), sum(own)
    return jnp.where((sub >= first) & (sub < first + count), value, 0.0)


def add(a, b):
    return b if a is None else a if b is None else a + b


def first_vector(new, coef, mask, x, tile, z, first_row, last_row):
    rows = slice(z, z + 8)
    west, east = coef[0, x, rows, :], coef[1, x, rows, :]
    south, north = coef[2, x, rows, :], coef[3, x, rows, :]
    middle = jnp.ones((8, 128), f32)
    middle = middle if first_row else middle + west
    middle = middle if last_row else middle + east
    terms = [None] * 9
    for label in range(3):
        term = where_own(label, z, middle)
        term = add(term, where_own(label, z - 1, cut(south, z, EDGES[label])))
        terms[3 + label] = add(term, where_own(label, z + 1, cut(north, z, EDGES[label] - 1)))
        if first_row:
            terms[label] = where_own(label, z, west)
        if last_row:
            terms[6 + label] = where_own(label, z, east)
    finish(terms, new, mask, x, tile, rows)


def smooth_vector(old, new, coef, mask, x, tile, z, first_row, last_row):
    rows = slice(z, z + 8)
    west, east = coef[0, x, rows, :], coef[1, x, rows, :]
    south, north = coef[2, x, rows, :], coef[3, x, rows, :]
    souths = [cut(south, z, edge) for edge in EDGES]
    norths = [cut(north, z, edge - 1) for edge in EDGES]
    terms = []
    for dx in SIDES:
        for label in range(3):
            at = 3 * (dx + 1) + label
            term = old[at, x, rows, :]
            if not first_row:
                term = term + west * old[at, x - 1, rows, :]
            elif dx < 1:
                term = term + west * old[at + 3, x - 1, rows, :]
            if not last_row:
                term = term + east * old[at, x + 1, rows, :]
            elif dx > -1:
                term = term + east * old[at - 3, x + 1, rows, :]
            term = term + souths[label] * old[at, x, z - 1 : z + 7, :]
            term = term + norths[label] * old[at, x, z + 1 : z + 9, :]
            terms.append(term)
    finish(terms, new, mask, x, tile, rows)


def iterate(vector, rim):
    def row(x, tile, first_row=False, last_row=False):
        for m in range(9):
            vector(x, tile, PAD - RIM + 8 * m, first_row, last_row)

    def rows(begin, end, tile):
        def step(x, carry):
            row(x, tile)
            return carry

        lax.fori_loop(begin, end, step, 0)

    rows(RIM - rim, RIM - 1, 0)
    row(RIM - 1, 0, last_row=True)
    row(RIM, 1, first_row=True)

    def inner(x, carry):
        row(x, jnp.where(x < RIM + 16, 1, 2))
        return carry

    lax.fori_loop(RIM + 1, RIM + 31, inner, 0)
    row(RIM + 31, 2, last_row=True)
    row(RIM + 32, 3, first_row=True)
    rows(RIM + 33, RIM + 32 + rim, 3)


def turn_tile(values, staged, part, dx, label, tc):
    z = PAD + 16 * tc
    region = 1 + tc // 2
    dy = side_of(label, region)
    cells = [values[3 * (dx + 1) + label, RIM + 8 * part + u, z : z + 16, :] for u in range(8)]
    turned = jnp.concatenate(cells, axis=0).T
    t = 6 * (2 * (1 - dx) + part // 2) + 2 * (1 - dy) + tc % 2
    for band in range(BANDS):
        q = 2 * band - 2 + region + dy
        if 0 <= q < 4:
            at = (8 * t + 4 * (part % 2) + q) * LANE_PITCH
            staged[at : at + LANE_PITCH, :] = turned[LANE_PITCH * band : LANE_PITCH * (band + 1)]


def gather_tiles(staged, out, begin, end, tr):
    def block(step, carry):
        for u in range(4):
            p = 4 * step + u
            for side in range(3):
                for b in range(6):
                    t = 6 * (2 * side + tr) + b
                    out[p, side, tr, 8 * b : 8 * b + 8, :] = staged[
                        pl.ds(8 * t * LANE_PITCH + p + side, 8, stride=LANE_PITCH), :
                    ]
        return carry

    lax.fori_loop(begin // 4, end // 4, block, 0)


def last_iteration(old, new, coef, mask, staged, out, out_hbm, sem, blocks):
    jobs = [(dx, label, tc) for dx in SIDES for label in range(3) for tc in range(4)]
    copies = []
    for part in range(5):
        if part < 4:
            for u in range(8):
                x = RIM + 8 * part + u
                for m in range(8):
                    smooth_vector(
                        old, new, coef, mask, x, 1 + part // 2, PAD + 8 * m, x == RIM, x == RIM + 31
                    )
                if part > 0:
                    for job in jobs[36 * u // 8 : 36 * (u + 1) // 8]:
                        turn_tile(new, staged, part - 1, *job)
        else:
            for job in jobs:
                turn_tile(new, staged, part - 1, *job)
        if part in (2, 4):
            tr = part // 2 - 1
            for side in range(2):
                begin, end = side * blocks // 2, (side + 1) * blocks // 2
                gather_tiles(staged, out, begin, end, tr)
                copy = pltpu.make_async_copy(
                    out.at[begin:end, :, tr], out_hbm.at[begin:end, :, tr], sem.at[2 * tr + side]
                )
                copy.start()
                copies.append(copy)
    for copy in copies:
        copy.wait()


def main_kernel(
    field_hbm, sup_ref, low_ref, high_ref, out_hbm,
    field, sup, cells, turned, mask, coef, values, other, staged, out, sem,
):
    rows = field_hbm.shape[1]
    blocks = sup_ref.shape[1]
    copies = [
        pltpu.make_async_copy(
            field_hbm.at[band], field.at[pl.ds(band * FIELD_ROWS + HALO, rows), :], sem.at[band]
        )
        for band in range(BANDS)
    ]
    for copy in copies:
        copy.start()
    for q in range(10):
        at = q * SUP_PITCH
        sup[at + 3 : at + 3 + blocks, :] = sup_ref[q]
        sup[at + 6 + blocks : at + SUP_PITCH, :] = jnp.zeros((SUP_PITCH - 6 - blocks, 128), f32)
    rest = FIELD_ROWS - rows - 2 * HALO
    for band in range(BANDS):
        at = band * FIELD_ROWS + rows + 2 * HALO
        field[at : at + rest, :] = jnp.zeros((rest, 128), f32)
    lane = lax.broadcasted_iota(jnp.int32, (HALO, 128), 1)
    for ref, at in ((low_ref, 0), (high_ref, HALO + rows)):
        left, right = ref[:HALO, :], ref[HALO : 2 * HALO, :]
        field[at : at + HALO, :] = left
        at = at + FIELD_ROWS
        field[at : at + HALO, :] = jnp.where(lane < 64, pltpu.roll(left, 64, 1), pltpu.roll(right, 64, 1))
        at = at + FIELD_ROWS
        field[at : at + HALO, :] = right
    for q in range(10):
        at = q * SUP_PITCH
        sup[at : at + 3, :] = low_ref[2 * HALO + 4 * q + 1 : 2 * HALO + 4 * q + 4, :]
        sup[at + 3 + blocks : at + 6 + blocks, :] = high_ref[2 * HALO + 4 * q : 2 * HALO + 4 * q + 3, :]
    turn_support(sup, turned)
    for copy in copies:
        copy.wait()
    build_cells(field, cells)
    build_masks(cells, turned, mask)
    build_faces(cells, coef)
    iterate(functools.partial(first_vector, other, coef, mask), ITERS - 1)
    old, new = other, values
    for count in range(1, ITERS - 1):
        iterate(functools.partial(smooth_vector, old, new, coef, mask), ITERS - 1 - count)
        old, new = new, old
    last_iteration(old, new, coef, mask, staged, out, out_hbm, sem, blocks)


def smooth(field, sup, low, high):
    blocks = sup.shape[1]
    vmem = pl.BlockSpec(memory_space=pltpu.VMEM)
    hbm = pl.BlockSpec(memory_space=pl.ANY)
    return pl.pallas_call(
        main_kernel,
        out_shape=jax.ShapeDtypeStruct((blocks, 3, 2, 48, 128), f32),
        in_specs=[hbm, vmem, vmem, vmem],
        out_specs=hbm,
        scratch_shapes=[
            pltpu.VMEM((BANDS * FIELD_ROWS, 128), f32),
            pltpu.VMEM((10 * SUP_PITCH, 128), f32),
            pltpu.VMEM((HIGH, PITCH, 128), f32),
            pltpu.VMEM((5, 6, 40, 128), f32),
            pltpu.VMEM((4, 9, PITCH, 128), f32),
            pltpu.VMEM((4, HIGH, PITCH, 128), f32),
            pltpu.VMEM((9, HIGH, PITCH, 128), f32),
            pltpu.VMEM((9, HIGH, PITCH, 128), f32),
            pltpu.VMEM((LANE_PITCH * BLOCK_ROWS, 128), f32),
            pltpu.VMEM((blocks, 3, 2, 48, 128), f32),
            pltpu.SemaphoreType.DMA((4,)),
        ],
        compiler_params=pltpu.CompilerParams(vmem_limit_bytes=60 * 1024 * 1024),
        name="smooth",
    )(field, sup, low, high)


def neighbours(up, down, axis):
    count = lax.axis_size(axis)
    forward = [(i, i + 1) for i in range(count - 1)]
    backward = [(i + 1, i) for i in range(count - 1)]
    return lax.ppermute(up, axis, forward), lax.ppermute(down, axis, backward)


def body(permeability, support):
    up, down = pack(permeability, support)
    from_left, from_right = neighbours(up, down, "gy")
    up, down = edges(permeability, support, from_left, from_right)
    low, high = neighbours(up, down, "gx")
    field, sup = widen(permeability, support, from_left, from_right)
    tiles = smooth(field, sup, low, high).reshape(support.shape[0], 36, 2, 4, 128)
    return tiles.transpose(0, 3, 1, 2, 4).reshape(support.shape + (256,))


def solution(mesh):
    return jax.shard_map(
        body,
        mesh=mesh,
        in_specs=(P(("grp", "gx"), "gy"), P(("grp", "gx"), "gy", None)),
        out_specs=P(("grp", "gx"), "gy", None, None),
        check_vma=False,
    )
```

```python
import functools

import jax
import jax.numpy as jnp
from jax import lax
from jax.experimental import pallas as pl
from jax.experimental.pallas import tpu as pltpu
from jax.sharding import PartitionSpec as P

ITERS = 4
SIDES = (-1, 0, 1)
TINY = 1e-30
OFF = 2.0

RIM = 4
PAD = 8
HIGH = 32 + 2 * RIM
PITCH = 64 + 2 * PAD
BANDS = 3
LANE_PITCH = 40
HALO = 40
WIDTH = 32 + RIM
FIELD_ROWS = 32 * LANE_PITCH + 16
SUP_PITCH = 48
BLOCK_ROWS = 36 * 8

f32 = jnp.float32


def cost(amount):
    return pl.CostEstimate(flops=amount, bytes_accessed=amount, transcendentals=0)


def support_rows(sup_ref):
    pad = jnp.zeros((sup_ref.shape[0], 92), f32)
    return [jnp.concatenate([sup_ref[:, q, :].astype(f32), pad], axis=1) for q in range(4)]


def groups_of(rows):
    third = -(-rows // 24) * 8
    return [(g, g * third, min(third, rows - g * third)) for g in range(3)]


def pack_kernel(perm_ref, sup_ref, up_ref, down_ref):
    rows = perm_ref.shape[0]
    parts = groups_of(rows)
    third = parts[0][2]
    lane = lax.broadcasted_iota(jnp.int32, (third, 128), 1)
    up = down = None
    for g, start, count in parts:
        part = perm_ref[start : start + count, :]
        if count < third:
            part = jnp.concatenate([part, jnp.zeros((third - count, 128), f32)], axis=0)
        high = pltpu.roll(part, WIDTH * (g + 1), 1)
        low = part if g == 0 else pltpu.roll(part, WIDTH * g, 1)
        up = high if up is None else jnp.where(lane < WIDTH * g, up, high)
        down = low if down is None else jnp.where(lane < WIDTH * g, down, low)
    up_ref[:third, :] = up
    down_ref[:third, :] = down
    wide = support_rows(sup_ref)
    up_ref[third:, :] = wide[1] + pltpu.roll(wide[2], 36, 1) + pltpu.roll(wide[3], 72, 1)
    down_ref[third:, :] = wide[0] + pltpu.roll(wide[1], 36, 1) + pltpu.roll(wide[2], 72, 1)


def pack(perm, support):
    third = groups_of(perm.shape[0])[0][2]
    shape = jax.ShapeDtypeStruct((third + support.shape[0], 128), f32)
    return pl.pallas_call(pack_kernel, out_shape=(shape, shape), name="pack")(perm, support)


def bands_of(own, left, right, g):
    lane = lax.broadcasted_iota(jnp.int32, own.shape, 1)
    moved = pltpu.roll(own, WIDTH, 1)
    if g > 0:
        left = pltpu.roll(left, 128 - WIDTH * g, 1)
    if g != 1:
        right = pltpu.roll(right, (128 + WIDTH - WIDTH * g) % 128, 1)
    return (
        jnp.where(lane < WIDTH, left, moved),
        pltpu.roll(own, 64 + WIDTH, 1),
        jnp.where(lane < WIDTH, moved, jnp.where(lane < 2 * WIDTH, right, 0.0)),
    )


def wide_support(sup_ref, left, right):
    shift = [0, 128 - 36, 128 - 72]
    low = [pltpu.roll(left, by, 1) if by else left for by in shift]
    high = [pltpu.roll(right, by, 1) if by else right for by in shift]
    return low + support_rows(sup_ref) + high


def edge_kernel(perm_ref, sup_ref, left_ref, right_ref, up_ref, down_ref):
    rows, blocks = perm_ref.shape[0], sup_ref.shape[0]
    groups = groups_of(rows)
    third = groups[0][2]
    for ref, g, start, block in ((up_ref, 2, rows - HALO, blocks - 4), (down_ref, 0, 0, 0)):
        packed = slice(start - groups[g][1], start - groups[g][1] + HALO)
        bands = bands_of(perm_ref[start : start + HALO, :], left_ref[packed, :], right_ref[packed, :], g)
        ref[:HALO, :] = bands[0]
        ref[HALO : 2 * HALO, :] = bands[2]
        four = slice(third + block, third + block + 4)
        wide = wide_support(sup_ref.at[pl.ds(block, 4)], left_ref[four, :], right_ref[four, :])
        for q in range(10):
            ref[2 * HALO + 4 * q : 2 * HALO + 4 * q + 4, :] = wide[q]


def edges(perm, support, from_left, from_right):
    edge = jax.ShapeDtypeStruct((2 * HALO + 40, 128), f32)
    return pl.pallas_call(
        edge_kernel, out_shape=(edge, edge), cost_estimate=cost(100_000), name="edges"
    )(perm, support, from_left, from_right)


def widen_kernel(perm_ref, sup_ref, left_ref, right_ref, field_ref, wide_ref):
    rows = perm_ref.shape[0]
    groups = groups_of(rows)
    third = groups[0][2]
    for g, start, count in groups:
        bands = bands_of(
            perm_ref[start : start + count, :], left_ref[:count, :], right_ref[:count, :], g
        )
        for band in range(BANDS):
            field_ref[band, start : start + count, :] = bands[band]
    for q, wide in enumerate(wide_support(sup_ref, left_ref[third:, :], right_ref[third:, :])):
        wide_ref[q] = wide


def widen(perm, support, from_left, from_right):
    rows, blocks = perm.shape[0], support.shape[0]
    return pl.pallas_call(
        widen_kernel,
        out_shape=(
            jax.ShapeDtypeStruct((BANDS, rows, 128), f32),
            jax.ShapeDtypeStruct((10, blocks, 128), f32),
        ),
        cost_estimate=cost(4_000_000),
        name="widen",
    )(perm, support, from_left, from_right)


def build_cells(field, cells):
    blank = jnp.zeros((128 - BANDS * LANE_PITCH, 128), f32)
    edge = jnp.zeros((PAD - RIM, 128), f32)

    def row(step, carry):
        for u in range(10):
            x = 10 * step + u
            parts = [
                field[pl.ds(band * FIELD_ROWS + 256 * m + x + HALO - WIDTH, 8, stride=32), :]
                for band in range(BANDS)
                for m in range(LANE_PITCH // 8)
            ]
            turned = jnp.concatenate(parts + [blank], axis=0).T
            cells[x, 0 : PAD - RIM, :] = edge
            cells[x, PAD - RIM : PITCH - PAD + RIM, :] = turned[: 64 + 2 * RIM]
            cells[x, PITCH - PAD + RIM : PITCH, :] = edge
        return carry

    lax.fori_loop(0, HIGH // 10, row, 0)


PIECES = (
    (PAD - RIM, RIM, 0, 1),
    (PAD, 16, 1, 0),
    (PAD + 16, 16, 1, 1),
    (PAD + 32, 16, 2, 0),
    (PAD + 48, 16, 2, 1),
    (PAD + 64, RIM, 3, 0),
)


def side_of(label, region):
    return (label - region + 1) % 3 - 1


def turn_support(sup, turned):
    blank = jnp.zeros((128 - BANDS * LANE_PITCH, 128), f32)
    for ex in range(5):
        for ey in range(6):
            parts = [
                sup[(2 * band + ey) * SUP_PITCH + ex : (2 * band + ey) * SUP_PITCH + ex + LANE_PITCH, :]
                for band in range(BANDS)
            ]
            turned[ex, ey] = jnp.concatenate(parts + [blank], axis=0).T[:40]


def build_masks(cells, turned, mask):
    for tile, (x, rx, tr) in enumerate(
        ((RIM - 1, 0, 1), (RIM, 1, 0), (RIM + 16, 1, 1), (RIM + 32, 2, 0))
    ):
        for start, count, region, tc in PIECES:
            inside = cells[x, start : start + 1, :] > 0.0
            for dx in SIDES:
                for label in range(3):
                    dy = side_of(label, region)
                    if dx == 0 and dy == 0:
                        on = inside
                    else:
                        t = 6 * (2 * (1 - dx) + tr) + 2 * (1 - dy) + tc
                        on = inside & (turned[rx + dx + 1, region + dy + 1, t : t + 1, :] == 1.0)
                    mask[tile, 3 * (dx + 1) + label, start : start + count, :] = jnp.broadcast_to(
                        jnp.where(on, f32(1.0), f32(0.0)), (count, 128)
                    )


def build_faces(cells, coef):
    starts = [PAD - RIM + 8 * m for m in range(9)]
    zero = jnp.zeros((8, 128), f32)
    sub = lax.broadcasted_iota(jnp.int32, (8, 128), 0)

    def face(p, q):
        return 2.0 * p * q / jnp.maximum(p + q, TINY)

    def row(x, west):
        east, south = [], []
        for z in starts:
            here = cells[x, z : z + 8, :]
            east.append(face(here, cells[x + 1, z : z + 8, :]))
            south.append(face(here, cells[x, z - 1 : z + 7, :]))
        for m, z in enumerate(starts):
            after = south[m + 1] if m < 8 else zero
            north = jnp.where(sub == 7, pltpu.roll(after, 7, 0), pltpu.roll(south[m], 7, 0))
            scale = OFF / jnp.maximum(west[m] + east[m] + south[m] + north, TINY)
            coef[0, x, z : z + 8, :] = scale * west[m]
            coef[1, x, z : z + 8, :] = scale * east[m]
            coef[2, x, z : z + 8, :] = scale * south[m]
            coef[3, x, z : z + 8, :] = scale * north
        return tuple(east)

    first = tuple(face(cells[0, z : z + 8, :], cells[1, z : z + 8, :]) for z in starts)
    lax.fori_loop(1, HIGH - 1, row, first)


def cut(field, z, edge):
    if not z <= edge < z + 8:
        return field
    sub = lax.broadcasted_iota(jnp.int32, (8, 128), 0)
    return jnp.where(sub == edge - z, 0.0, field)


EDGES = (PAD + 32, PAD + 64, PAD)


def region_of(z):
    return 0 if z < PAD else 3 if z >= PAD + 64 else 1 + (z - PAD) // 32


def finish(terms, new, mask, x, tile, rows):
    total = None
    for at, term in enumerate(terms):
        if term is not None:
            terms[at] = term = mask[tile, at, rows, :] * term
            total = term if total is None else total + term
    inverse = 1.0 / jnp.maximum(total, TINY)
    for at, term in enumerate(terms):
        new[at, x, rows, :] = jnp.zeros((8, 128), f32) if term is None else term * inverse


def where_own(label, z, value):
    own = [side_of(label, region_of(z + i)) == 0 for i in range(8)]
    if all(own):
        return value
    if not any(own):
        return None
    sub = lax.broadcasted_iota(jnp.int32, (8, 128), 0)
    first, count = own.index(True), sum(own)
    return jnp.where((sub >= first) & (sub < first + count), value, 0.0)


def add(a, b):
    return b if a is None else a if b is None else a + b


def first_vector(new, coef, mask, x, tile, z, first_row, last_row):
    rows = slice(z, z + 8)
    west, east = coef[0, x, rows, :], coef[1, x, rows, :]
    south, north = coef[2, x, rows, :], coef[3, x, rows, :]
    middle = jnp.ones((8, 128), f32)
    middle = middle if first_row else middle + west
    middle = middle if last_row else middle + east
    terms = [None] * 9
    for label in range(3):
        term = where_own(label, z, middle)
        term = add(term, where_own(label, z - 1, cut(south, z, EDGES[label])))
        terms[3 + label] = add(term, where_own(label, z + 1, cut(north, z, EDGES[label] - 1)))
        if first_row:
            terms[label] = where_own(label, z, west)
        if last_row:
            terms[6 + label] = where_own(label, z, east)
    finish(terms, new, mask, x, tile, rows)


def smooth_vector(old, new, coef, mask, x, tile, z, first_row, last_row):
    rows = slice(z, z + 8)
    west, east = coef[0, x, rows, :], coef[1, x, rows, :]
    south, north = coef[2, x, rows, :], coef[3, x, rows, :]
    souths = [cut(south, z, edge) for edge in EDGES]
    norths = [cut(north, z, edge - 1) for edge in EDGES]
    terms = []
    for dx in SIDES:
        for label in range(3):
            at = 3 * (dx + 1) + label
            term = old[at, x, rows, :]
            if not first_row:
                term = term + west * old[at, x - 1, rows, :]
            elif dx < 1:
                term = term + west * old[at + 3, x - 1, rows, :]
            if not last_row:
                term = term + east * old[at, x + 1, rows, :]
            elif dx > -1:
                term = term + east * old[at - 3, x + 1, rows, :]
            term = term + souths[label] * old[at, x, z - 1 : z + 7, :]
            term = term + norths[label] * old[at, x, z + 1 : z + 9, :]
            terms.append(term)
    finish(terms, new, mask, x, tile, rows)


def iterate(vector, rim):
    def row(x, tile, first_row=False, last_row=False):
        for m in range(9):
            vector(x, tile, PAD - RIM + 8 * m, first_row, last_row)

    def rows(begin, end, tile):
        def step(x, carry):
            row(x, tile)
            return carry

        lax.fori_loop(begin, end, step, 0)

    rows(RIM - rim, RIM - 1, 0)
    row(RIM - 1, 0, last_row=True)
    row(RIM, 1, first_row=True)

    def inner(x, carry):
        row(x, jnp.where(x < RIM + 16, 1, 2))
        return carry

    lax.fori_loop(RIM + 1, RIM + 31, inner, 0)
    row(RIM + 31, 2, last_row=True)
    row(RIM + 32, 3, first_row=True)
    rows(RIM + 33, RIM + 32 + rim, 3)


def turn_tile(values, staged, part, dx, label, tc):
    z = PAD + 16 * tc
    region = 1 + tc // 2
    dy = side_of(label, region)
    cells = [values[3 * (dx + 1) + label, RIM + 8 * part + u, z : z + 16, :] for u in range(8)]
    turned = jnp.concatenate(cells, axis=0).T
    t = 6 * (2 * (1 - dx) + part // 2) + 2 * (1 - dy) + tc % 2
    for band in range(BANDS):
        q = 2 * band - 2 + region + dy
        if 0 <= q < 4:
            at = (8 * t + 4 * (part % 2) + q) * LANE_PITCH
            staged[at : at + LANE_PITCH, :] = turned[LANE_PITCH * band : LANE_PITCH * (band + 1)]


def gather_tiles(staged, out, begin, end, tr):
    def block(step, carry):
        for u in range(4):
            p = 4 * step + u
            for side in range(3):
                for b in range(6):
                    t = 6 * (2 * side + tr) + b
                    out[p, side, tr, 8 * b : 8 * b + 8, :] = staged[
                        pl.ds(8 * t * LANE_PITCH + p + side, 8, stride=LANE_PITCH), :
                    ]
        return carry

    lax.fori_loop(begin // 4, end // 4, block, 0)


def last_iteration(old, new, coef, mask, staged, out, out_hbm, sem, blocks):
    jobs = [(dx, label, tc) for dx in SIDES for label in range(3) for tc in range(4)]
    copies = []
    for part in range(5):
        if part < 4:
            for u in range(8):
                x = RIM + 8 * part + u
                for m in range(8):
                    smooth_vector(
                        old, new, coef, mask, x, 1 + part // 2, PAD + 8 * m, x == RIM, x == RIM + 31
                    )
                if part > 0:
                    for job in jobs[36 * u // 8 : 36 * (u + 1) // 8]:
                        turn_tile(new, staged, part - 1, *job)
        else:
            for job in jobs:
                turn_tile(new, staged, part - 1, *job)
        if part in (2, 4):
            tr = part // 2 - 1
            for side in range(2):
                begin, end = side * blocks // 2, (side + 1) * blocks // 2
                gather_tiles(staged, out, begin, end, tr)
                copy = pltpu.make_async_copy(
                    out.at[begin:end, :, tr], out_hbm.at[begin:end, :, tr], sem.at[2 * tr + side]
                )
                copy.start()
                copies.append(copy)
    for copy in copies:
        copy.wait()


def main_kernel(
    field_hbm, sup_ref, low_ref, high_ref, out_hbm,
    field, sup, cells, turned, mask, coef, values, other, staged, out, sem,
):
    rows = field_hbm.shape[1]
    blocks = sup_ref.shape[1]
    copies = [
        pltpu.make_async_copy(
            field_hbm.at[band], field.at[pl.ds(band * FIELD_ROWS + HALO, rows), :], sem.at[band]
        )
        for band in range(BANDS)
    ]
    for copy in copies:
        copy.start()
    for q in range(10):
        at = q * SUP_PITCH
        sup[at + 3 : at + 3 + blocks, :] = sup_ref[q]
        sup[at + 6 + blocks : at + SUP_PITCH, :] = jnp.zeros((SUP_PITCH - 6 - blocks, 128), f32)
    rest = FIELD_ROWS - rows - 2 * HALO
    for band in range(BANDS):
        at = band * FIELD_ROWS + rows + 2 * HALO
        field[at : at + rest, :] = jnp.zeros((rest, 128), f32)
    lane = lax.broadcasted_iota(jnp.int32, (HALO, 128), 1)
    for ref, at in ((low_ref, 0), (high_ref, HALO + rows)):
        left, right = ref[:HALO, :], ref[HALO : 2 * HALO, :]
        field[at : at + HALO, :] = left
        at = at + FIELD_ROWS
        field[at : at + HALO, :] = jnp.where(lane < 64, pltpu.roll(left, 64, 1), pltpu.roll(right, 64, 1))
        at = at + FIELD_ROWS
        field[at : at + HALO, :] = right
    for q in range(10):
        at = q * SUP_PITCH
        sup[at : at + 3, :] = low_ref[2 * HALO + 4 * q + 1 : 2 * HALO + 4 * q + 4, :]
        sup[at + 3 + blocks : at + 6 + blocks, :] = high_ref[2 * HALO + 4 * q : 2 * HALO + 4 * q + 3, :]
    turn_support(sup, turned)
    for copy in copies:
        copy.wait()
    build_cells(field, cells)
    build_masks(cells, turned, mask)
    build_faces(cells, coef)
    iterate(functools.partial(first_vector, other, coef, mask), ITERS - 1)
    old, new = other, values
    for count in range(1, ITERS - 1):
        iterate(functools.partial(smooth_vector, old, new, coef, mask), ITERS - 1 - count)
        old, new = new, old
    last_iteration(old, new, coef, mask, staged, out, out_hbm, sem, blocks)


def smooth(field, sup, low, high):
    blocks = sup.shape[1]
    vmem = pl.BlockSpec(memory_space=pltpu.VMEM)
    hbm = pl.BlockSpec(memory_space=pl.ANY)
    return pl.pallas_call(
        main_kernel,
        out_shape=jax.ShapeDtypeStruct((blocks, 3, 2, 48, 128), f32),
        in_specs=[hbm, vmem, vmem, vmem],
        out_specs=hbm,
        scratch_shapes=[
            pltpu.VMEM((BANDS * FIELD_ROWS + 32, 128), f32),
            pltpu.VMEM((10 * SUP_PITCH, 128), f32),
            pltpu.VMEM((HIGH, PITCH, 128), f32),
            pltpu.VMEM((5, 6, 40, 128), f32),
            pltpu.VMEM((4, 9, PITCH, 128), f32),
            pltpu.VMEM((4, HIGH, PITCH, 128), f32),
            pltpu.VMEM((9, HIGH, PITCH, 128), f32),
            pltpu.VMEM((9, HIGH, PITCH, 128), f32),
            pltpu.VMEM((LANE_PITCH * (BLOCK_ROWS + 1), 128), f32),
            pltpu.VMEM((blocks, 3, 2, 48, 128), f32),
            pltpu.SemaphoreType.DMA((4,)),
        ],
        compiler_params=pltpu.CompilerParams(vmem_limit_bytes=60 * 1024 * 1024),
        name="smooth",
    )(field, sup, low, high)


def neighbours(up, down, axis):
    count = lax.axis_size(axis)
    forward = [(i, i + 1) for i in range(count - 1)]
    backward = [(i + 1, i) for i in range(count - 1)]
    return lax.ppermute(up, axis, forward), lax.ppermute(down, axis, backward)


def body(permeability, support):
    up, down = pack(permeability, support)
    from_left, from_right = neighbours(up, down, "gy")
    up, down = edges(permeability, support, from_left, from_right)
    low, high = neighbours(up, down, "gx")
    field, sup = widen(permeability, support, from_left, from_right)
    tiles = smooth(field, sup, low, high).reshape(support.shape[0], 36, 2, 4, 128)
    return tiles.transpose(0, 3, 1, 2, 4).reshape(support.shape + (256,))


def solution(mesh):
    return jax.shard_map(
        body,
        mesh=mesh,
        in_specs=(P(("grp", "gx"), "gy"), P(("grp", "gx"), "gy", None)),
        out_specs=P(("grp", "gx"), "gy", None, None),
        check_vma=False,
    )
```
